128 devices in a mesh: ia: 2 (over z_hi), ja: 8 (over x, core), ka: 8 (over y, z_lo).
Axes of the slice: x: 4, y: 4, z: 4 (z_hi: 2, z_lo: 2; z = z_hi * 2 + z_lo), core: 2. Of those that a mesh axis runs over, the one named last changes fastest.
Arguments:
- hidden_act: bfloat16 [768, 26624], P(('ia', 'ka'), 'ja'), may hold values from -6 to 6
- w_down: bfloat16 [26624, 16384], P('ja', ('ia', 'ka')), may hold values from -0.0390625 to 0.0390625
- w_out: bfloat16 [16384, 16384], P(('ia', 'ka'), 'ja'), may hold values from -0.046875 to 0.046875
- head_grad: bfloat16 [768, 16384], P(('ia', 'ka'), 'ja'), may hold values from -6 to 6
- token_ratio: float32 [768], P(('ia', 'ka')), may hold values from -4 to 4
- pair_slot: int32 [768], P(('ia', 'ka')), may hold values from 0 to 15
- segment_id: int32 [768], P(('ia', 'ka')), may hold values from 0 to 191, never falling along the last dimension, each value on 1 to 16 neighbouring positions
Outputs:
- projected: bfloat16 [768, 16384], P(('ia', 'ka'), 'ja')
- grad_hidden: bfloat16 [768, 26624], P(('ia', 'ka'), 'ja')
- grad_down: bfloat16 [26624, 16384], P('ja', ('ia', 'ka'))
- grad_out: bfloat16 [16384, 16384], P(('ia', 'ka'), 'ja')
The draws below stay inside these ranges and needn't reach their ends.
All inputs are finite; a program needn't handle non-finite values.
Results may differ from the reference program's by a relative error of at most 0.0058.
Values may be sent and summed in bfloat16 or wider, within the bound.
A program may use at most 128 MiB of HBM per device.

```python
import math
import jax
import jax.numpy as jnp
import numpy as np
from jax import lax

D = 16384
FF = 26624
PAIRS = 8
TOKENS = 768
SEGS = 192
SEG_MOST = 16


def set_ends(drawn, stream_key, low, top_value):
    longest = drawn.shape.index(max(drawn.shape))
    spots = []
    for shift in (0, 1):
        where = [jax.random.randint(jax.random.fold_in(stream_key, axis), (), 0, length) for axis, length in enumerate(drawn.shape)]
        where[longest] = (where[longest] + shift) % drawn.shape[longest]
        spots.append(tuple(where))
    return drawn.at[spots[0]].set(low).at[spots[1]].set(top_value)


def level_of(stream_key, dims, pieces, low, high):
    def one(axis_at, shards_of):
        steps = jax.random.uniform(jax.random.fold_in(jax.random.fold_in(stream_key, 6), axis_at), (shards_of,), jnp.float32, low / len(pieces), high / len(pieces))
        return jnp.repeat(jnp.exp(steps), dims[axis_at] // shards_of).reshape((-1,) + (1,) * (len(dims) - axis_at - 1))

    level = one(*pieces[0])
    for cut in pieces[1:]:
        level = level * one(*cut)
    return level


def split_up(number_of, total, bound, skew):
    loads = [(1 << 20) // math.isqrt(standing ** skew) + 1 for standing in range(2, number_of + 1)]
    rest, given = total - bound - (number_of - 1), [1] * (number_of - 1)
    while rest > 0:
        movable = [i for i in range(number_of - 1) if given[i] < bound]
        whole, remaining = sum([loads[i] for i in movable]), rest
        for i in movable:
            more = min(bound - given[i], max(1, remaining * loads[i] // whole), rest)
            given[i] = given[i] + more
            rest = rest - more
    return np.array([bound] + given)


def ragged_sizes(own_key, amount, total, most, slope):
    if amount == 2:
        one = jax.random.randint(own_key, (), max(1, total - most), min(most, total - 1) + 1)
        return jnp.stack([one, total - one])
    tallies = jnp.asarray(split_up(amount, total, most, slope), jnp.int32)
    pairs = (amount - 1) // 2
    giver, sink = tallies[1:1 + 2 * pairs:2], tallies[2:2 + 2 * pairs:2]
    slack = jnp.minimum(giver - 1, most - sink)
    passed = jax.random.randint(jax.random.fold_in(own_key, 1), (pairs,), 0, 1 << 20) % (slack + 1)
    tallies = tallies.at[1:1 + 2 * pairs:2].set(giver - passed).at[2:2 + 2 * pairs:2].set(sink + passed)
    return tallies[jax.random.permutation(jax.random.fold_in(own_key, 2), amount)]


def noise(rng, extent, spread, reach, pieces=(), kind=jnp.bfloat16):
    entries = spread * jax.random.normal(rng, extent, jnp.float32)
    if pieces:
        entries = entries * level_of(rng, extent, pieces, -0.22, 0.18)
    return jnp.clip(entries, -reach, reach).astype(kind)


def setup_inputs(seed: int = 0) -> dict:
    arg_keys = jax.random.split(jax.random.key(seed), 8)
    hidden_act = noise(arg_keys[0], (TOKENS, FF), 1.0, 6.0, ((0, 16), (1, 8)))
    w_down = noise(arg_keys[1], (FF, D), FF ** -0.5, 0.0390625, ((0, 8), (1, 16)))
    w_out = noise(arg_keys[2], (D, D), D ** -0.5, 0.046875, ((0, 16), (1, 8)))
    head_grad = noise(arg_keys[3], (TOKENS, D), 1.0, 6.0, ((0, 16), (1, 8)))
    token_ratio = noise(arg_keys[4], (TOKENS,), 0.5, 4.0, ((0, 16),), jnp.float32)
    pair_slot = set_ends(jax.random.randint(arg_keys[5], (TOKENS,), 0, 2 * PAIRS), jax.random.fold_in(arg_keys[5], 1), 0, (2 * PAIRS) - 1).astype(jnp.int32)
    segment_id = jnp.searchsorted(jnp.cumsum(ragged_sizes(arg_keys[6], SEGS, TOKENS, SEG_MOST, 1)), jnp.arange(TOKENS), side="right").astype(jnp.int32)
    return dict(hidden_act=hidden_act, w_down=w_down, w_out=w_out, head_grad=head_grad, token_ratio=token_ratio, pair_slot=pair_slot, segment_id=segment_id)


beta_scale = 0.5


def reference(hidden_act, w_down, w_out, head_grad, token_ratio, pair_slot, segment_id):
    down_out = jnp.dot(hidden_act, w_down, preferred_element_type=jnp.float32).astype(jnp.bfloat16)
    projected = jnp.dot(down_out, w_out, preferred_element_type=jnp.float32).astype(jnp.bfloat16)
    masked = (segment_id % 2).astype(jnp.float32)
    signed = masked * (1 - 2 * (pair_slot % 2)).astype(jnp.float32)
    onehot = ((pair_slot // 2)[:, None] == jnp.arange(PAIRS, dtype=jnp.int32)[None, :]).astype(jnp.float32)
    margin = jnp.dot(signed * token_ratio, onehot, precision=lax.Precision.HIGHEST)
    pair_weight = -beta_scale * jax.nn.sigmoid(-beta_scale * margin)
    coef = jnp.dot(onehot, pair_weight, precision=lax.Precision.HIGHEST) * signed
    cotangent = (coef[:, None] * head_grad.astype(jnp.float32)).astype(jnp.bfloat16)
    grad_mid = jnp.dot(cotangent, w_out.T, preferred_element_type=jnp.float32).astype(jnp.bfloat16)
    grad_out = jnp.dot(down_out.T, cotangent, preferred_element_type=jnp.float32).astype(jnp.bfloat16)
    grad_hidden = jnp.dot(grad_mid, w_down.T, preferred_element_type=jnp.float32).astype(jnp.bfloat16)
    grad_down = jnp.dot(hidden_act.T, grad_mid, preferred_element_type=jnp.float32).astype(jnp.bfloat16)
    return (projected, grad_hidden, grad_down, grad_out)
```

```python
import functools

import jax
import jax.numpy as jnp
from jax import lax
from jax.experimental import pallas as pl
from jax.experimental.pallas import tpu as pltpu
from jax.sharding import PartitionSpec as P

PAIRS = 8
MESH = pl.DeviceIdType.MESH
BF = jnp.bfloat16
F32 = jnp.float32

beta_scale = 0.5


def dot_nt(a, b):
    return lax.dot_general(a, b, (((1,), (1,)), ((), ())), preferred_element_type=F32)


def dot_nn(a, b):
    return lax.dot_general(a, b, (((1,), (0,)), ((), ())), preferred_element_type=F32)


def kernel(
    rows, tile_ref, hid_ref, wd_ref, wo_ref, hg_ref,
    proj_ref, gh_ref, gd_ref, go_ref,
    wd, wo, hid, hg, cot, tiles,
    sib_out, sib_in, part, xout, xin, gm, dn,
    g_out, g_in, g_acc, g_out2, g_in2, g_fin,
    p_out, p_in, p_acc, p_out2, p_in2, p_fin,
    stage, ssem, rsem, lsem, osem,
):
    ia, ja, ka = lax.axis_index("ia"), lax.axis_index("ja"), lax.axis_index("ka")
    z, y, x, core = ia * 2 + ka % 2, ka // 2, ja // 2, ja % 2

    def peer(dx=0, dc=0, dy=0, dz=0):
        pz, py, px, pc = (z + dz) % 4, (y + dy) % 4, (x + dx) % 4, (core + dc) % 2
        return (pz // 2, px * 2 + pc, py * 2 + pz % 2)

    count = [0]
    sent = []

    def send(src, dst, **where):
        i = count[0]
        count[0] += 1
        copy = pltpu.make_async_remote_copy(
            src, dst, ssem.at[i], rsem.at[i], device_id=peer(**where), device_id_type=MESH
        )
        copy.start()
        sent.append(copy)
        return copy

    def finish(copies):
        for copy in copies:
            copy.wait_send()
            sent[:] = [other for other in sent if other is not copy]

    def arrive(copies):
        for copy in copies:
            copy.wait_recv()

    near = (2, 1, 3)

    loads = [
        pltpu.make_async_copy(hg_ref, hg.at[0, 0], lsem.at[0]),
        pltpu.make_async_copy(hid_ref, hid.at[0, 0], lsem.at[1]),
        pltpu.make_async_copy(tile_ref, tiles.at[0, 0], lsem.at[2]),
        pltpu.make_async_copy(wo_ref, wo, lsem.at[3]),
        pltpu.make_async_copy(wd_ref, wd, lsem.at[4]),
    ]
    for load in loads:
        load.start()

    barrier = pltpu.get_barrier_semaphore()
    peers = [dict(dc=1)] + [{a: d} for a in ("dx", "dy", "dz") for d in near]
    for where in peers:
        pl.semaphore_signal(barrier, inc=1, device_id=peer(**where), device_id_type=MESH)
    pl.semaphore_wait(barrier, len(peers))
    for load in loads[:3]:
        load.wait()

    def gather_first(full):
        half = full.shape[3] // 2
        lo, hi = pl.ds(0, half), pl.ds(half, half)
        first = [
            send(full.at[0, 0, :, lo], full.at[0, (4 - d) % 4, :, lo], dy=d) for d in near
        ]
        other = [
            send(full.at[0, 0, :, hi], full.at[(4 - d) % 4, 0, :, hi], dz=d) for d in near
        ]
        return first, other

    def gather_second(full, first, other):
        half = full.shape[3] // 2
        lo, hi = pl.ds(0, half), pl.ds(half, half)
        arrive(first)
        copies = [
            send(full.at[0, :, :, lo], full.at[(4 - d) % 4, :, :, lo], dz=d) for d in near
        ]
        arrive(other)
        return copies + [
            send(full.at[:, 0, :, hi], full.at[:, (4 - d) % 4, :, hi], dy=d) for d in near
        ]

    tile_first = [send(tiles.at[0, 0], tiles.at[0, (4 - d) % 4], dy=d) for d in near]
    hg_first = gather_first(hg)
    hid_first = gather_first(hid)
    arrive(tile_first)
    tile_second = [send(tiles.at[0], tiles.at[(4 - d) % 4], dz=d) for d in near]
    hg_second = gather_second(hg, *hg_first)
    hid_second = gather_second(hid, *hid_first)

    arrive(tile_second)
    margin = jnp.sum(tiles[:, :, 0:rows, :], axis=(0, 1, 2))[None, :]
    weight = -beta_scale * jax.nn.sigmoid(-beta_scale * margin)

    arrive(hg_second)

    def scale(i, _):
        coef = jnp.sum(tiles[i // 4, i % 4, rows:, :] * weight, axis=1, keepdims=True)
        cot[i // 4, i % 4] = (coef * hg[i // 4, i % 4].astype(F32)).astype(BF)
        return 0

    lax.fori_loop(0, 16, scale, 0)

    tokens = 16 * rows
    quarter = 4 * rows
    d1 = wd.shape[1]
    half1 = d1 // 2

    def reduce_start(term, dest):
        def tile_of(which, ref):
            def body(j, _):
                start = pl.multiple_of(which * half1 + j * 256, 256)
                value = term(start)
                ref[:, :, pl.ds(pl.multiple_of(j * 256, 256), 256)] = value.reshape(4, quarter, 256)
                return 0

            lax.fori_loop(0, half1 // 256, body, 0)

        tile_of(1 - core, sib_out)
        swap = send(sib_out, sib_in, dc=1)
        tile_of(core, part)
        return swap

    def reduce_x(swap):
        arrive([swap])

        def body(i, _):
            total = part[i] + sib_in[i]
            part[i] = total
            xout[i] = total.astype(BF)
            return 0

        lax.fori_loop(0, 4, body, 0)
        return [send(xout.at[(x + d) % 4], xin.at[d - 1], dx=d) for d in near]

    def reduce_sum(moves, dest):
        arrive(moves)
        total = part[x]
        for d in range(3):
            total = total + xin[d].astype(F32)
        dest[core, x] = total.astype(BF)
        return [send(dest.at[core, x], dest.at[core, x], dx=d) for d in near]

    def reduce_relay(moves, dest):
        arrive(moves)
        return send(dest.at[core], dest.at[core], dc=1)

    loads[3].wait()

    def back_term(start):
        return dot_nt(cot[...].reshape(tokens, -1), wo[pl.ds(start, 256), :])

    swap = reduce_start(back_term, gm)
    moves = reduce_x(swap)
    loads[4].wait()
    spread = reduce_sum(moves, gm)
    relay = reduce_relay(spread, gm)
    arrive([relay])
    finish([swap, *moves])

    def block_rows(full, axis, d):
        out = []
        for h in range(2):
            if axis == "z":
                out.append(full[h, d])
            else:
                out.append(
                    jnp.concatenate([full[h, i, d * rows:(d + 1) * rows] for i in range(4)], axis=0)
                )
        return out

    def scatter_first(full, mult, o, inn, acc):
        copies = []
        for d in near:
            for s, axis in enumerate("zy"):
                left = block_rows(full, axis, d)
                o[s, d - 1] = mult(s, left).astype(BF)
                copies.append(send(o.at[s, d - 1], inn.at[s, d - 1], **{"d" + axis: d}))
        for s, axis in enumerate("zy"):
            acc[s] = mult(s, block_rows(full, axis, 0))
        return copies

    def scatter_second(copies, inn, acc, o2, in2):
        arrive(copies)
        out = []

        def summed(s, b):
            where = pl.ds(b * rows, rows)
            total = acc[s, where]
            for d in range(3):
                total = total + inn[s, d, where].astype(F32)
            return total

        for s, axis in enumerate("yz"):
            for d in near:
                o2[s, d - 1] = summed(s, d).astype(BF)
                out.append(send(o2.at[s, d - 1], in2.at[s, d - 1], **{"d" + axis: d}))
        for s in range(2):
            acc[s, 0:rows] = summed(s, 0)
        return out

    def scatter_last(copies, acc, in2, fin, ref, sem):
        arrive(copies)
        half = acc.shape[2]
        for s in range(2):
            total = acc[s, 0:rows]
            for d in range(3):
                total = total + in2[s, d].astype(F32)
            fin[:, s * half:(s + 1) * half] = total.astype(BF)
        copy = pltpu.make_async_copy(fin, ref, sem)
        copy.start()
        return copy

    ff = wd.shape[0]
    d2 = wo.shape[1]

    def hidden_mult(s, left):
        cols = slice(s * (ff // 2), (s + 1) * (ff // 2))
        return dot_nt(left[0], wd[cols, 0:half1]) + dot_nt(left[1], wd[cols, half1:])

    def out_mult(s, left):
        cols = slice(s * (d2 // 2), (s + 1) * (d2 // 2))
        return dot_nn(left[0], wo[0:half1, cols]) + dot_nn(left[1], wo[half1:, cols])

    g_first = scatter_first(gm, hidden_mult, g_out, g_in, g_acc)

    arrive(hid_second)

    def down_term(start):
        return dot_nn(hid[...].reshape(tokens, -1), wd[:, pl.ds(start, 256)])

    swap = reduce_start(down_term, dn)
    moves = reduce_x(swap)

    def weight_rows(left, right, ref, first, last):
        def out_copy(i, slot):
            return pltpu.make_async_copy(
                stage.at[slot, :, 0:ref.shape[1]], ref.at[pl.ds(pl.multiple_of(i * 256, 256), 256)], osem.at[slot]
            )

        def body(i, _):
            slot = i % 2

            @pl.when(i >= first + 2)
            def _():
                out_copy(i - 2, slot).wait()

            value = right(left(i).T)
            stage[slot, :, 0:ref.shape[1]] = value.astype(BF)
            out_copy(i, slot).start()
            return 0

        lax.fori_loop(first, last, body, 0)
        for i in (last - 2, last - 1):
            out_copy(i, i % 2).wait()

    def hid_cols(i):
        return hid[:, :, :, pl.ds(pl.multiple_of(i * 256, 256), 256)].reshape(tokens, 256)

    def times_gm(left):
        return jnp.concatenate(
            [dot_nn(left, gm[h].reshape(tokens, half1)) for h in range(2)], axis=1
        )

    blocks = ff // 256
    weight_rows(hid_cols, times_gm, gd_ref, 0, 4)
    spread = reduce_sum(moves, dn)
    weight_rows(hid_cols, times_gm, gd_ref, 4, 8)
    relay2 = reduce_relay(spread, dn)
    g_second = scatter_second(g_first, g_in, g_acc, g_out2, g_in2)
    arrive([relay2])
    p_first = scatter_first(dn, out_mult, p_out, p_in, p_acc)
    g_done = scatter_last(g_second, g_acc, g_in2, g_fin, gh_ref, lsem.at[5])

    per = half1 // 256

    def dn_cols(i):
        return dn[i // per, :, :, pl.ds(pl.multiple_of((i % per) * 256, 256), 256)].reshape(tokens, 256)

    def times_cot(left):
        return dot_nn(left, cot[...].reshape(tokens, d2))

    weight_rows(hid_cols, times_gm, gd_ref, 8, blocks)
    weight_rows(dn_cols, times_cot, go_ref, 0, 2)
    p_second = scatter_second(p_first, p_in, p_acc, p_out2, p_in2)
    weight_rows(dn_cols, times_cot, go_ref, 2, d1 // 256)
    p_done = scatter_last(p_second, p_acc, p_in2, p_fin, proj_ref, lsem.at[6])
    g_done.wait()
    p_done.wait()
    finish(list(sent))


def local(hidden_act, w_down, w_out, head_grad, token_ratio, pair_slot, segment_id):
    rows, ff = hidden_act.shape
    d1 = w_down.shape[1]
    d2 = w_out.shape[1]
    half1 = d1 // 2
    quarter = 4 * rows

    signed = (segment_id % 2).astype(F32) * (1 - 2 * (pair_slot % 2)).astype(F32)
    onehot = ((pair_slot // 2)[:, None] == jnp.arange(128, dtype=jnp.int32)[None, :]).astype(F32)
    tile = jnp.concatenate(
        [onehot * (signed * token_ratio)[:, None], onehot * signed[:, None]], axis=0
    )

    def reduce_shapes(width):
        half = width // 2
        return [
            pltpu.VMEM((2, 3, quarter, half), BF),
            pltpu.VMEM((2, 3, quarter, half), BF),
            pltpu.VMEM((2, quarter, half), F32),
            pltpu.VMEM((2, 3, rows, half), BF),
            pltpu.VMEM((2, 3, rows, half), BF),
            pltpu.VMEM((rows, width), BF),
        ]

    anywhere = pl.BlockSpec(memory_space=pl.ANY)
    copies = 80
    return pl.pallas_call(
        functools.partial(kernel, rows),
        out_shape=(
            jax.ShapeDtypeStruct((rows, d2), BF),
            jax.ShapeDtypeStruct((rows, ff), BF),
            jax.ShapeDtypeStruct((ff, d1), BF),
            jax.ShapeDtypeStruct((d1, d2), BF),
        ),
        in_specs=[anywhere] * 5,
        out_specs=[anywhere] * 4,
        scratch_shapes=[
            pltpu.VMEM((ff, d1), BF),
            pltpu.VMEM((d1, d2), BF),
            pltpu.VMEM((4, 4, rows, ff), BF),
            pltpu.VMEM((4, 4, rows, d2), BF),
            pltpu.VMEM((4, 4, rows, d2), BF),
            pltpu.VMEM((4, 4, 2 * rows, 128), F32),
            pltpu.VMEM((4, quarter, half1), F32),
            pltpu.VMEM((4, quarter, half1), F32),
            pltpu.VMEM((4, quarter, half1), F32),
            pltpu.VMEM((4, quarter, half1), BF),
            pltpu.VMEM((3, quarter, half1), BF),
            pltpu.VMEM((2, 4, quarter, half1), BF),
            pltpu.VMEM((2, 4, quarter, half1), BF),
            *reduce_shapes(ff),
            *reduce_shapes(d2),
            pltpu.VMEM((2, 256, d2), BF),
            pltpu.SemaphoreType.DMA((copies,)),
            pltpu.SemaphoreType.DMA((copies,)),
            pltpu.SemaphoreType.DMA((8,)),
            pltpu.SemaphoreType.DMA((2,)),
        ],
        compiler_params=pltpu.CompilerParams(
            collective_id=0, has_side_effects=True, vmem_limit_bytes=62 << 20
        ),
        cost_estimate=pl.CostEstimate(
            flops=6 * 16 * rows * d1 * (ff + d2),
            bytes_accessed=4 * d1 * (ff + d2),
            transcendentals=128,
        ),
    )(tile, hidden_act, w_down, w_out, head_grad)


def solution(mesh):
    placed = (
        P(("ia", "ka"), "ja"),
        P("ja", ("ia", "ka")),
        P(("ia", "ka"), "ja"),
        P(("ia", "ka"), "ja"),
        P(("ia", "ka")),
        P(("ia", "ka")),
        P(("ia", "ka")),
    )
    return jax.shard_map(
        local,
        mesh=mesh,
        in_specs=placed,
        out_specs=(
            P(("ia", "ka"), "ja"),
            P(("ia", "ka"), "ja"),
            P("ja", ("ia", "ka")),
            P(("ia", "ka"), "ja"),
        ),
        check_vma=False,
    )
```

```python
import functools

import jax
import jax.numpy as jnp
from jax import lax
from jax.experimental import pallas as pl
from jax.experimental.pallas import tpu as pltpu
from jax.sharding import PartitionSpec as P

PAIRS = 8
MESH = pl.DeviceIdType.MESH
BF = jnp.bfloat16
F32 = jnp.float32

beta_scale = 0.5


def dot_nt(a, b):
    return lax.dot_general(a, b, (((1,), (1,)), ((), ())), preferred_element_type=F32)


def dot_nn(a, b):
    return lax.dot_general(a, b, (((1,), (0,)), ((), ())), preferred_element_type=F32)


def kernel(
    rows, tile_ref, hid_ref, wd_ref, wo_ref, hg_ref,
    proj_ref, gh_ref, gd_ref, go_ref,
    wd, wo, hid, hg, cot, tiles,
    sib_out, sib_in, part, xout, xin, gm, dn,
    *bufs,
):
    g_bufs, p_bufs, (stage, ssem, rsem, lsem, osem) = bufs[:8], bufs[8:16], bufs[16:]
    ia, ja, ka = lax.axis_index("ia"), lax.axis_index("ja"), lax.axis_index("ka")
    z, y, x, core = ia * 2 + ka % 2, ka // 2, ja // 2, ja % 2

    def peer(dx=0, dc=0, dy=0, dz=0):
        pz, py, px, pc = (z + dz) % 4, (y + dy) % 4, (x + dx) % 4, (core + dc) % 2
        return (pz // 2, px * 2 + pc, py * 2 + pz % 2)

    count = [0]
    sent = []

    def send(src, dst, **where):
        i = count[0]
        count[0] += 1
        copy = pltpu.make_async_remote_copy(
            src, dst, ssem.at[i], rsem.at[i], device_id=peer(**where), device_id_type=MESH
        )
        copy.start()
        sent.append(copy)
        return copy

    def finish(copies):
        for copy in copies:
            copy.wait_send()
            sent[:] = [other for other in sent if other is not copy]

    def arrive(copies):
        for copy in copies:
            copy.wait_recv()

    near = (2, 1, 3)

    loads = [
        pltpu.make_async_copy(hg_ref, hg.at[0, 0], lsem.at[0]),
        pltpu.make_async_copy(hid_ref, hid.at[0, 0], lsem.at[1]),
        pltpu.make_async_copy(tile_ref, tiles.at[0, 0], lsem.at[2]),
        pltpu.make_async_copy(wo_ref, wo, lsem.at[3]),
        pltpu.make_async_copy(wd_ref, wd, lsem.at[4]),
    ]
    for load in loads:
        load.start()

    barrier = pltpu.get_barrier_semaphore()
    peers = [dict(dc=1)] + [{a: d} for a in ("dx", "dy", "dz") for d in near]
    for where in peers:
        pl.semaphore_signal(barrier, inc=1, device_id=peer(**where), device_id_type=MESH)
    pl.semaphore_wait(barrier, len(peers))
    for load in loads[:3]:
        load.wait()

    class Gather:
        def __init__(self, full):
            self.full = full
            self.width = full.shape[3] // 2
            self.cut = self.width // 2 // 128 * 128
            self.got = {}

        def columns(self, s, part=None):
            base = s * self.width
            if part is None:
                return pl.ds(base, self.width)
            return pl.ds(base, self.cut) if part == 0 else pl.ds(base + self.cut, self.width - self.cut)

        def slot(self, s, p, q, part=None):
            cols = self.columns(s, part)
            return self.full.at[q, p, :, cols] if s == 0 else self.full.at[p, q, :, cols]

        def along(self, s, second, sign):
            return {("dy", "dz")[(s + second) % 2]: sign}

        def take(self, *key):
            arrive([self.got.pop(key)])

        def start_first(self):
            for sign in (1, -1):
                for s in (0, 1):
                    self.got["p", s, sign] = send(
                        self.slot(s, 0, 0), self.slot(s, -sign % 4, 0), **self.along(s, 0, sign)
                    )

        def across(self, s, p):
            for sign in (1, -1):
                self.got["s", s, p, sign] = send(
                    self.slot(s, p, 0), self.slot(s, p, -sign % 4), **self.along(s, 1, sign)
                )

        def start_second(self):
            for s in (0, 1):
                self.across(s, 0)

        def hand_on(self):
            for sign in (1, -1):
                for s in (0, 1):
                    self.take("p", s, sign)
                    part = 0 if sign == 1 else 1
                    self.got["f", s, sign] = send(
                        self.slot(s, -sign % 4, 0, part), self.slot(s, 2, 0, part), **self.along(s, 0, sign)
                    )
            for sign in (1, -1):
                for s in (0, 1):
                    self.across(s, -sign % 4)

        def far(self):
            for s in (0, 1):
                self.take("f", s, 1)
                self.take("f", s, -1)
                self.across(s, 2)

        def hand_across(self, p):
            for sign in (1, -1):
                for s in (0, 1):
                    self.take("s", s, p, sign)
                    self.take("s", s, p + 1, sign)
                    part = 0 if sign == 1 else 1
                    self.got["g", s, p, sign] = send(
                        self.slot(s, pl.ds(p, 2), -sign % 4, part),
                        self.slot(s, pl.ds(p, 2), 2, part),
                        **self.along(s, 1, sign),
                    )

        def done(self):
            for key in list(self.got):
                self.take(*key)

    grad_rows, hidden_rows = Gather(hg), Gather(hid)
    tile_first = [send(tiles.at[0, 0], tiles.at[0, (4 - d) % 4], dy=d) for d in near]
    grad_rows.start_first()
    grad_rows.start_second()
    hidden_rows.start_first()
    arrive(tile_first)
    tile_second = [send(tiles.at[0], tiles.at[(4 - d) % 4], dz=d) for d in near]
    grad_rows.hand_on()
    grad_rows.far()
    hidden_rows.start_second()
    grad_rows.hand_across(0)
    grad_rows.hand_across(2)
    hidden_rows.hand_on()
    hidden_rows.far()

    arrive(tile_second)
    margin = jnp.sum(tiles[:, :, 0:rows, :], axis=(0, 1, 2))[None, :]
    weight = -beta_scale * jax.nn.sigmoid(-beta_scale * margin)

    grad_rows.done()

    def scale(i, _):
        coef = jnp.sum(tiles[i // 4, i % 4, rows:, :] * weight, axis=1, keepdims=True)
        cot[i // 4, i % 4] = (coef * hg[i // 4, i % 4].astype(F32)).astype(BF)
        return 0

    lax.fori_loop(0, 16, scale, 0)

    tokens = 16 * rows
    quarter = 4 * rows
    d1 = wd.shape[1]
    half1 = d1 // 2

    def partial_sum(term, which, ref):
        def body(j, _):
            value = term(pl.multiple_of(which * half1 + j * 256, 256))
            ref[:, :, pl.ds(pl.multiple_of(j * 256, 256), 256)] = value.reshape(4, quarter, 256)
            return 0

        lax.fori_loop(0, half1 // 256, body, 0)

    def reduce_x(swap):
        arrive([swap])

        def body(i, _):
            total = part[i] + sib_in[i]
            part[i] = total
            xout[i] = total.astype(BF)
            return 0

        lax.fori_loop(0, 4, body, 0)
        return [send(xout.at[(x + d) % 4], xin.at[d - 1], dx=d) for d in near]

    def reduce_sum(moves, dest):
        arrive(moves)
        total = part[x]
        for d in range(3):
            total = total + xin[d].astype(F32)
        dest[core, x] = total.astype(BF)
        return [send(dest.at[core, x], dest.at[core, x], dx=d) for d in near]

    def reduce_relay(moves, dest):
        arrive(moves)
        return send(dest.at[core], dest.at[core], dc=1)

    loads[3].wait()

    def back_term(start):
        return dot_nt(cot[...].reshape(tokens, -1), wo[pl.ds(start, 256), :])

    partial_sum(back_term, 1 - core, sib_out)
    swap = send(sib_out, sib_in, dc=1)
    hidden_rows.hand_across(0)
    partial_sum(back_term, core, part)
    hidden_rows.hand_across(2)
    moves = reduce_x(swap)
    loads[4].wait()
    spread = reduce_sum(moves, gm)
    finish([swap, *moves])
    hidden_rows.done()

    def down_term(start):
        return dot_nn(hid[...].reshape(tokens, -1), wd[:, pl.ds(start, 256)])

    partial_sum(down_term, 1 - core, sib_out)
    relay = reduce_relay(spread, gm)
    arrive([relay])
    swap = send(sib_out, sib_in, dc=1)

    def block_rows(full, axis, d):
        out = []
        for h in range(2):
            if axis == "z":
                out.append(full[h, d])
            else:
                out.append(
                    jnp.concatenate([full[h, i, d * rows:(d + 1) * rows] for i in range(4)], axis=0)
                )
        return out

    class Scatter:
        def __init__(self, full, mult, acc, out, relay, inn, out2, relay2, inn2, fin):
            self.full, self.mult, self.acc, self.fin = full, mult, acc, fin
            self.stages = ((out, relay, inn), (out2, relay2, inn2))
            self.width = acc.shape[2]
            cut = self.width // 2 // 128 * 128
            self.parts = (slice(0, cut), slice(cut, self.width))
            self.got = {}

        def axis(self, s, stage):
            return "zy"[(s + stage) % 2]

        def term(self, s, stage, d, part):
            if stage == 0:
                return self.mult(s, block_rows(self.full, self.axis(s, 0), d), part)
            return self.acc[s, d * rows:(d + 1) * rows, part]

        def move(self, key, s, stage, d, part, value, dst, sign):
            out = self.stages[stage][0]
            cols = pl.ds(part.start, part.stop - part.start)
            out[s, d - 1, :, part] = value.astype(BF)
            self.got[key, s, stage, sign] = send(
                out.at[s, d - 1, :, cols], dst.at[:, cols], **{"d" + self.axis(s, stage): sign}
            )

        def take(self, key, s, stage, sign):
            arrive([self.got.pop((key, s, stage, sign))])

        def far(self, s, stage):
            relay = self.stages[stage][1]
            for part, sign in zip(self.parts, (1, -1)):
                self.move("relay", s, stage, 2, part, self.term(s, stage, 2, part), relay.at[s], sign)

        def direct(self, s, stage):
            inn = self.stages[stage][2]
            for part, sign in zip(self.parts[::-1], (1, -1)):
                d = sign % 4
                self.move("direct", s, stage, d, part, self.term(s, stage, d, part), inn.at[s, d // 2], sign)

        def joined(self, s, stage):
            relay, inn = self.stages[stage][1:]
            for part, sign in zip(self.parts, (1, -1)):
                d = sign % 4
                value = self.term(s, stage, d, part)
                self.take("relay", s, stage, sign)
                value = value + relay[s, :, part].astype(F32)
                self.move("joined", s, stage, d, part, value, inn.at[s, d // 2], sign)

        def own(self, s):
            for part in self.parts:
                self.acc[s, :, part] = self.term(s, 0, 0, part)

        def total(self, s):
            inn = self.stages[0][2]
            for key in ("direct", "joined"):
                for sign in (1, -1):
                    self.take(key, s, 0, sign)
            self.acc[s] = self.acc[s] + inn[s, 0].astype(F32) + inn[s, 1].astype(F32)

        def last(self, ref, sem):
            inn = self.stages[1][2]
            for s in (0, 1):
                for key in ("direct", "joined"):
                    for sign in (1, -1):
                        self.take(key, s, 1, sign)
                value = self.acc[s, 0:rows] + inn[s, 0].astype(F32) + inn[s, 1].astype(F32)
                self.fin[:, s * self.width:(s + 1) * self.width] = value.astype(BF)
            copy = pltpu.make_async_copy(self.fin, ref, sem)
            copy.start()
            return copy

    ff = wd.shape[0]
    d2 = wo.shape[1]

    def hidden_mult(s, left, part):
        cols = slice(s * (ff // 2) + part.start, s * (ff // 2) + part.stop)
        return dot_nt(left[0], wd[cols, 0:half1]) + dot_nt(left[1], wd[cols, half1:])

    def out_mult(s, left, part):
        cols = slice(s * (d2 // 2) + part.start, s * (d2 // 2) + part.stop)
        return dot_nn(left[0], wo[0:half1, cols]) + dot_nn(left[1], wo[half1:, cols])

    grad_hidden = Scatter(gm, hidden_mult, *g_bufs)
    projected = Scatter(dn, out_mult, *p_bufs)
    hid_blocks = ff // 256

    def weight_rows(left, right, ref, first, last):
        def out_copy(i, slot):
            return pltpu.make_async_copy(
                stage.at[slot, :, 0:ref.shape[1]], ref.at[pl.ds(pl.multiple_of(i * 256, 256), 256)], osem.at[slot]
            )

        def body(i, _):
            slot = i % 2

            @pl.when(i >= first + 2)
            def _():
                out_copy(i - 2, slot).wait()

            value = right(left(i).T)
            stage[slot, :, 0:ref.shape[1]] = value.astype(BF)
            out_copy(i, slot).start()
            return 0

        lax.fori_loop(first, last, body, 0)
        for i in (last - 2, last - 1):
            out_copy(i, i % 2).wait()

    def hid_cols(i):
        return hid[:, :, :, pl.ds(pl.multiple_of(i * 256, 256), 256)].reshape(tokens, 256)

    def times_gm(left):
        return jnp.concatenate(
            [dot_nn(left, gm[h].reshape(tokens, half1)) for h in range(2)], axis=1
        )

    per = half1 // 256

    def dn_cols(i):
        return dn[i // per, :, :, pl.ds(pl.multiple_of((i % per) * 256, 256), 256)].reshape(tokens, 256)

    def times_cot(left):
        return dot_nn(left, cot[...].reshape(tokens, d2))

    def down_rows(first, last):
        weight_rows(hid_cols, times_gm, gd_ref, first, last)

    def out_rows(first, last):
        weight_rows(dn_cols, times_cot, go_ref, first, last)

    for s in (0, 1):
        grad_hidden.far(s, 0)
    partial_sum(down_term, core, part)
    moves = reduce_x(swap)
    for s in (0, 1):
        grad_hidden.direct(s, 0)
    for s in (0, 1):
        grad_hidden.joined(s, 0)
    for s in (0, 1):
        grad_hidden.own(s)
    down_rows(0, 2)
    spread = reduce_sum(moves, dn)
    down_rows(2, 8)
    for s in (0, 1):
        grad_hidden.total(s)
        grad_hidden.far(s, 1)
    for s in (0, 1):
        grad_hidden.direct(s, 1)
    relay2 = reduce_relay(spread, dn)
    for s in (0, 1):
        grad_hidden.joined(s, 1)
    arrive([relay2])
    for s in (0, 1):
        projected.far(s, 0)
    for s in (0, 1):
        projected.direct(s, 0)
    g_done = grad_hidden.last(gh_ref, lsem.at[5])
    down_rows(8, 10)
    for s in (0, 1):
        projected.joined(s, 0)
    for s in (0, 1):
        projected.own(s)
    down_rows(10, hid_blocks)
    for s in (0, 1):
        projected.total(s)
        projected.far(s, 1)
    for s in (0, 1):
        projected.direct(s, 1)
    out_rows(0, 2)
    for s in (0, 1):
        projected.joined(s, 1)
    out_rows(2, d1 // 256)
    p_done = projected.last(proj_ref, lsem.at[6])
    g_done.wait()
    p_done.wait()
    finish(list(sent))


def local(hidden_act, w_down, w_out, head_grad, token_ratio, pair_slot, segment_id):
    rows, ff = hidden_act.shape
    d1 = w_down.shape[1]
    d2 = w_out.shape[1]
    half1 = d1 // 2
    quarter = 4 * rows

    signed = (segment_id % 2).astype(F32) * (1 - 2 * (pair_slot % 2)).astype(F32)
    onehot = ((pair_slot // 2)[:, None] == jnp.arange(128, dtype=jnp.int32)[None, :]).astype(F32)
    tile = jnp.concatenate(
        [onehot * (signed * token_ratio)[:, None], onehot * signed[:, None]], axis=0
    )

    def reduce_shapes(width):
        half = width // 2
        shapes = [pltpu.VMEM((2, quarter, half), F32)]
        for count in (quarter, rows):
            shapes += [
                pltpu.VMEM((2, 3, count, half), BF),
                pltpu.VMEM((2, count, half), BF),
                pltpu.VMEM((2, 2, count, half), BF),
            ]
        return shapes + [pltpu.VMEM((rows, width), BF)]

    anywhere = pl.BlockSpec(memory_space=pl.ANY)
    copies = 144
    return pl.pallas_call(
        functools.partial(kernel, rows),
        out_shape=(
            jax.ShapeDtypeStruct((rows, d2), BF),
            jax.ShapeDtypeStruct((rows, ff), BF),
            jax.ShapeDtypeStruct((ff, d1), BF),
            jax.ShapeDtypeStruct((d1, d2), BF),
        ),
        in_specs=[anywhere] * 5,
        out_specs=[anywhere] * 4,
        scratch_shapes=[
            pltpu.VMEM((ff, d1), BF),
            pltpu.VMEM((d1, d2), BF),
            pltpu.VMEM((4, 4, rows, ff), BF),
            pltpu.VMEM((4, 4, rows, d2), BF),
            pltpu.VMEM((4, 4, rows, d2), BF),
            pltpu.VMEM((4, 4, 2 * rows, 128), F32),
            pltpu.VMEM((4, quarter, half1), F32),
            pltpu.VMEM((4, quarter, half1), F32),
            pltpu.VMEM((4, quarter, half1), F32),
            pltpu.VMEM((4, quarter, half1), BF),
            pltpu.VMEM((3, quarter, half1), BF),
            pltpu.VMEM((2, 4, quarter, half1), BF),
            pltpu.VMEM((2, 4, quarter, half1), BF),
            *reduce_shapes(ff),
            *reduce_shapes(d2),
            pltpu.VMEM((2, 256, d2), BF),
            pltpu.SemaphoreType.DMA((copies,)),
            pltpu.SemaphoreType.DMA((copies,)),
            pltpu.SemaphoreType.DMA((8,)),
            pltpu.SemaphoreType.DMA((2,)),
        ],
        compiler_params=pltpu.CompilerParams(
            collective_id=0, has_side_effects=True, vmem_limit_bytes=62 << 20
        ),
        cost_estimate=pl.CostEstimate(
            flops=6 * 16 * rows * d1 * (ff + d2),
            bytes_accessed=4 * d1 * (ff + d2),
            transcendentals=128,
        ),
    )(tile, hidden_act, w_down, w_out, head_grad)


def solution(mesh):
    placed = (
        P(("ia", "ka"), "ja"),
        P("ja", ("ia", "ka")),
        P(("ia", "ka"), "ja"),
        P(("ia", "ka"), "ja"),
        P(("ia", "ka")),
        P(("ia", "ka")),
        P(("ia", "ka")),
    )
    return jax.shard_map(
        local,
        mesh=mesh,
        in_specs=placed,
        out_specs=(
            P(("ia", "ka"), "ja"),
            P(("ia", "ka"), "ja"),
            P("ja", ("ia", "ka")),
            P(("ia", "ka"), "ja"),
        ),
        check_vma=False,
    )
```

```python
import functools

import jax
import jax.numpy as jnp
from jax import lax
from jax.experimental import pallas as pl
from jax.experimental.pallas import tpu as pltpu
from jax.sharding import PartitionSpec as P

MESH = pl.DeviceIdType.MESH
BF = jnp.bfloat16
F32 = jnp.float32

beta_scale = 0.5


def dot_nt(a, b):
    return lax.dot_general(a, b, (((1,), (1,)), ((), ())), preferred_element_type=F32)


def dot_nn(a, b):
    return lax.dot_general(a, b, (((1,), (0,)), ((), ())), preferred_element_type=F32)


def kernel(
    rows, ratio_ref, slot_ref, segment_ref, hid_ref, wd_ref, wo_ref, hg_ref,
    proj_ref, gh_ref, gd_ref, go_ref,
    wd, wo, hid, hg, cot, tiles,
    sib_out, sib_in, part, xout, xin, gm, dn,
    *bufs,
):
    g_bufs, p_bufs, (stage, ssem, rsem, lsem, osem) = bufs[:8], bufs[8:16], bufs[16:]
    ia, ja, ka = lax.axis_index("ia"), lax.axis_index("ja"), lax.axis_index("ka")
    z, y, x, core = ia * 2 + ka % 2, ka // 2, ja // 2, ja % 2

    def peer(dx=0, dc=0, dy=0, dz=0):
        pz, py, px, pc = (z + dz) % 4, (y + dy) % 4, (x + dx) % 4, (core + dc) % 2
        return (pz // 2, px * 2 + pc, py * 2 + pz % 2)

    count = [0]
    sent = []

    def send(src, dst, **where):
        i = count[0]
        count[0] += 1
        copy = pltpu.make_async_remote_copy(
            src, dst, ssem.at[i], rsem.at[i], device_id=peer(**where), device_id_type=MESH
        )
        copy.start()
        sent.append(copy)
        return copy

    def finish(copies):
        for copy in copies:
            copy.wait_send()
            sent[:] = [other for other in sent if other is not copy]

    def arrive(copies):
        for copy in copies:
            copy.wait_recv()

    near = (2, 1, 3)

    loads = [
        pltpu.make_async_copy(hg_ref, hg.at[0, 0], lsem.at[0]),
        pltpu.make_async_copy(hid_ref, hid.at[0, 0], lsem.at[1]),
        pltpu.make_async_copy(wo_ref, wo, lsem.at[2]),
        pltpu.make_async_copy(wd_ref, wd, lsem.at[3]),
    ]
    for load in loads:
        load.start()

    sign = ((segment_ref[...] & 1) * (1 - 2 * (slot_ref[...] & 1))).astype(F32)
    tiles[0, 0] = jnp.full((8, 128), -1.0, F32)
    tiles[0, 0, 0:1, 0:rows] = sign * ratio_ref[...]
    tiles[0, 0, 1:2, 0:rows] = (slot_ref[...] >> 1).astype(F32)
    tiles[0, 0, 2:3, 0:rows] = sign

    barrier = pltpu.get_barrier_semaphore()
    peers = [dict(dc=1)] + [{a: d} for a in ("dx", "dy", "dz") for d in near]
    for where in peers:
        pl.semaphore_signal(barrier, inc=1, device_id=peer(**where), device_id_type=MESH)
    pl.semaphore_wait(barrier, len(peers))
    for load in loads[:2]:
        load.wait()

    class Gather:
        def __init__(self, full):
            self.full = full
            self.width = full.shape[3] // 2
            self.cut = self.width // 2 // 128 * 128
            self.got = {}

        def columns(self, s, part=None):
            base = s * self.width
            if part is None:
                return pl.ds(base, self.width)
            return pl.ds(base, self.cut) if part == 0 else pl.ds(base + self.cut, self.width - self.cut)

        def slot(self, s, p, q, part=None):
            cols = self.columns(s, part)
            return self.full.at[q, p, :, cols] if s == 0 else self.full.at[p, q, :, cols]

        def along(self, s, second, sign):
            return {("dy", "dz")[(s + second) % 2]: sign}

        def take(self, *key):
            arrive([self.got.pop(key)])

        def start_first(self):
            for sign in (1, -1):
                for s in (0, 1):
                    self.got["p", s, sign] = send(
                        self.slot(s, 0, 0), self.slot(s, -sign % 4, 0), **self.along(s, 0, sign)
                    )

        def across(self, s, p):
            for sign in (1, -1):
                self.got["s", s, p, sign] = send(
                    self.slot(s, p, 0), self.slot(s, p, -sign % 4), **self.along(s, 1, sign)
                )

        def start_second(self):
            for s in (0, 1):
                self.across(s, 0)

        def hand_on(self):
            for sign in (1, -1):
                for s in (0, 1):
                    self.take("p", s, sign)
                    part = 0 if sign == 1 else 1
                    self.got["f", s, sign] = send(
                        self.slot(s, -sign % 4, 0, part), self.slot(s, 2, 0, part), **self.along(s, 0, sign)
                    )
            for sign in (1, -1):
                for s in (0, 1):
                    self.across(s, -sign % 4)

        def far(self):
            for s in (0, 1):
                self.take("f", s, 1)
                self.take("f", s, -1)
                self.across(s, 2)

        def hand_across(self, p):
            for sign in (1, -1):
                for s in (0, 1):
                    self.take("s", s, p, sign)
                    self.take("s", s, p + 1, sign)
                    part = 0 if sign == 1 else 1
                    self.got["g", s, p, sign] = send(
                        self.slot(s, pl.ds(p, 2), -sign % 4, part),
                        self.slot(s, pl.ds(p, 2), 2, part),
                        **self.along(s, 1, sign),
                    )

        def done(self):
            for key in list(self.got):
                self.take(*key)

    grad_rows, hidden_rows = Gather(hg), Gather(hid)
    grad_rows.start_first()
    tile_first = [send(tiles.at[0, 0], tiles.at[0, (4 - d) % 4], dy=d) for d in near]
    grad_rows.start_second()
    hidden_rows.start_first()
    arrive(tile_first)
    tile_second = [send(tiles.at[0], tiles.at[(4 - d) % 4], dz=d) for d in near]
    grad_rows.hand_on()
    grad_rows.far()
    hidden_rows.start_second()
    grad_rows.hand_across(0)
    grad_rows.hand_across(2)

    arrive(tile_second)
    pairs = lax.broadcasted_iota(jnp.int32, (8, 128), 0).astype(F32)

    def add_margin(i, total):
        tile = tiles[i // 4, i % 4]
        return total + jnp.where(tile[1:2] == pairs, tile[0:1], 0.0)

    margin = jnp.sum(
        lax.fori_loop(0, 16, add_margin, jnp.zeros((8, 128), F32)), axis=1, keepdims=True
    )
    weight = -beta_scale * jax.nn.sigmoid(-beta_scale * margin)

    def scale(i, _):
        tile = tiles[i // 4, i % 4]
        line = jnp.sum(jnp.where(tile[1:2] == pairs, weight, 0.0), axis=0, keepdims=True) * tile[2:3]
        coef = jnp.broadcast_to(line, (8, 128)).T[0:rows, 0:1]
        cot[i // 4, i % 4] = (coef * hg[i // 4, i % 4].astype(F32)).astype(BF)
        return 0

    tokens = 16 * rows
    quarter = 4 * rows
    d1 = wd.shape[1]
    half1 = d1 // 2

    class Reduce:
        def __init__(self, term, dest):
            self.term, self.dest = term, dest
            self.swaps, self.moves, self.spread, self.relays = {}, {}, {}, {}

        def fill(self, j, which, ref):
            value = self.term(pl.multiple_of(which * half1 + j * 256, 256))
            ref[j] = value.reshape(4, quarter, 256)

        def theirs(self, j):
            self.fill(j, 1 - core, sib_out)

        def swap(self, j):
            self.swaps[j] = send(sib_out.at[j], sib_in.at[j], dc=1)

        def mine(self, j):
            self.fill(j, core, part)

        def start(self, j):
            arrive([self.swaps[j]])

            def body(i, _):
                total = part[j, i] + sib_in[j, i]
                part[j, i] = total
                xout[j, i] = total.astype(BF)
                return 0

            lax.fori_loop(0, 4, body, 0)
            self.moves[j] = [send(xout.at[j, (x + d) % 4], xin.at[j, d - 1], dx=d) for d in near]

        def sum(self, j):
            arrive(self.moves[j])
            finish([self.swaps[j]])
            total = part[j, x]
            for d in range(3):
                total = total + xin[j, d].astype(F32)
            cols = slice(j * 256, j * 256 + 256)
            self.dest[core, x, :, cols] = total.astype(BF)
            spot = self.dest.at[core, x, :, pl.ds(j * 256, 256)]
            self.spread[j] = [send(spot, spot, dx=d) for d in near]

        def relay(self, j):
            arrive(self.spread[j])
            spot = self.dest.at[core, :, :, pl.ds(j * 256, 256)]
            self.relays[j] = send(spot, spot, dc=1)

        def done(self, j):
            arrive([self.relays[j]])
            finish(self.moves[j])

    def back_term(start):
        return dot_nt(cot[...].reshape(tokens, -1), wo[pl.ds(start, 256), :])

    def down_term(start):
        return dot_nn(hid[...].reshape(tokens, -1), wd[:, pl.ds(start, 256)])

    sum_back, sum_down = Reduce(back_term, gm), Reduce(down_term, dn)

    grad_rows.done()
    hidden_rows.hand_on()
    lax.fori_loop(0, 16, scale, 0)
    loads[2].wait()
    sum_back.theirs(0)
    sum_back.swap(0)
    hidden_rows.far()
    sum_back.mine(0)
    sum_back.start(0)
    sum_back.theirs(1)
    sum_back.swap(1)
    hidden_rows.hand_across(0)
    sum_back.mine(1)
    sum_back.start(1)
    hidden_rows.hand_across(2)
    sum_back.sum(0)
    loads[3].wait()
    sum_back.sum(1)
    sum_back.relay(0)
    hidden_rows.done()
    sum_down.theirs(0)
    sum_back.done(0)
    sum_down.swap(0)
    sum_back.relay(1)
    sum_down.mine(0)
    sum_back.done(1)

    def block_rows(full, axis, d):
        out = []
        for h in range(2):
            if axis == "z":
                out.append(full[h, d])
            else:
                out.append(
                    jnp.concatenate([full[h, i, d * rows:(d + 1) * rows] for i in range(4)], axis=0)
                )
        return out

    class Scatter:
        def __init__(self, full, mult, acc, out, relay, inn, out2, relay2, inn2, fin):
            self.full, self.mult, self.acc, self.fin = full, mult, acc, fin
            self.stages = ((out, relay, inn), (out2, relay2, inn2))
            self.width = acc.shape[2]
            cut = self.width // 2 // 128 * 128
            self.parts = (slice(0, cut), slice(cut, self.width))
            self.got = {}

        def axis(self, s, stage):
            return "zy"[(s + stage) % 2]

        def term(self, s, stage, d, part):
            if stage == 0:
                return self.mult(s, block_rows(self.full, self.axis(s, 0), d), part)
            return self.acc[s, d * rows:(d + 1) * rows, part]

        def move(self, key, s, stage, d, part, value, dst, sign):
            out = self.stages[stage][0]
            cols = pl.ds(part.start, part.stop - part.start)
            out[s, d - 1, :, part] = value.astype(BF)
            self.got[key, s, stage, sign] = send(
                out.at[s, d - 1, :, cols], dst.at[:, cols], **{"d" + self.axis(s, stage): sign}
            )

        def take(self, key, s, stage, sign):
            arrive([self.got.pop((key, s, stage, sign))])

        def far(self, s, stage):
            relay = self.stages[stage][1]
            for part, sign in zip(self.parts, (1, -1)):
                self.move("relay", s, stage, 2, part, self.term(s, stage, 2, part), relay.at[s], sign)

        def direct(self, s, stage):
            inn = self.stages[stage][2]
            for part, sign in zip(self.parts[::-1], (1, -1)):
                d = sign % 4
                self.move("direct", s, stage, d, part, self.term(s, stage, d, part), inn.at[s, d // 2], sign)

        def joined(self, s, stage):
            relay, inn = self.stages[stage][1:]
            for part, sign in zip(self.parts, (1, -1)):
                d = sign % 4
                value = self.term(s, stage, d, part)
                self.take("relay", s, stage, sign)
                value = value + relay[s, :, part].astype(F32)
                self.move("joined", s, stage, d, part, value, inn.at[s, d // 2], sign)

        def own(self, s):
            for part in self.parts:
                self.acc[s, :, part] = self.term(s, 0, 0, part)

        def total(self, s):
            inn = self.stages[0][2]
            for key in ("direct", "joined"):
                for sign in (1, -1):
                    self.take(key, s, 0, sign)
            self.acc[s] = self.acc[s] + inn[s, 0].astype(F32) + inn[s, 1].astype(F32)

        def last(self, ref, sem):
            inn = self.stages[1][2]
            for s in (0, 1):
                for key in ("direct", "joined"):
                    for sign in (1, -1):
                        self.take(key, s, 1, sign)
                value = self.acc[s, 0:rows] + inn[s, 0].astype(F32) + inn[s, 1].astype(F32)
                self.fin[:, s * self.width:(s + 1) * self.width] = value.astype(BF)
            copy = pltpu.make_async_copy(self.fin, ref, sem)
            copy.start()
            return copy

    ff = wd.shape[0]
    d2 = wo.shape[1]

    def hidden_mult(s, left, part):
        cols = slice(s * (ff // 2) + part.start, s * (ff // 2) + part.stop)
        return dot_nt(left[0], wd[cols, 0:half1]) + dot_nt(left[1], wd[cols, half1:])

    def out_mult(s, left, part):
        cols = slice(s * (d2 // 2) + part.start, s * (d2 // 2) + part.stop)
        return dot_nn(left[0], wo[0:half1, cols]) + dot_nn(left[1], wo[half1:, cols])

    grad_hidden = Scatter(gm, hidden_mult, *g_bufs)
    projected = Scatter(dn, out_mult, *p_bufs)
    hid_blocks = ff // 256

    def weight_rows(left, right, ref, first, last):
        def out_copy(i, slot):
            return pltpu.make_async_copy(
                stage.at[slot, :, 0:ref.shape[1]], ref.at[pl.ds(pl.multiple_of(i * 256, 256), 256)], osem.at[slot]
            )

        def body(i, _):
            slot = i % 2

            @pl.when(i >= first + 2)
            def _():
                out_copy(i - 2, slot).wait()

            value = right(left(i).T)
            stage[slot, :, 0:ref.shape[1]] = value.astype(BF)
            out_copy(i, slot).start()
            return 0

        lax.fori_loop(first, last, body, 0)
        for i in (last - 2, last - 1):
            out_copy(i, i % 2).wait()

    def hid_cols(i):
        return hid[:, :, :, pl.ds(pl.multiple_of(i * 256, 256), 256)].reshape(tokens, 256)

    def times_gm(left):
        return jnp.concatenate(
            [dot_nn(left, gm[h].reshape(tokens, half1)) for h in range(2)], axis=1
        )

    per = half1 // 256

    def dn_cols(i):
        return dn[i // per, :, :, pl.ds(pl.multiple_of((i % per) * 256, 256), 256)].reshape(tokens, 256)

    def times_cot(left):
        return dot_nn(left, cot[...].reshape(tokens, d2))

    def down_rows(first, last):
        weight_rows(hid_cols, times_gm, gd_ref, first, last)

    def out_rows(first, last):
        weight_rows(dn_cols, times_cot, go_ref, first, last)

    sum_down.start(0)
    for s in (0, 1):
        grad_hidden.far(s, 0)
    sum_down.theirs(1)
    sum_down.swap(1)
    sum_down.mine(1)
    sum_down.start(1)
    for s in (0, 1):
        grad_hidden.direct(s, 0)
    sum_down.sum(0)
    for s in (0, 1):
        grad_hidden.joined(s, 0)
    sum_down.sum(1)
    for s in (0, 1):
        grad_hidden.own(s)
    down_rows(0, 2)
    sum_down.relay(0)
    down_rows(2, 4)
    sum_down.relay(1)
    sum_down.done(0)
    sum_down.done(1)
    for s in (0, 1):
        projected.far(s, 0)
    for s in (0, 1):
        projected.direct(s, 0)
    down_rows(4, 6)
    for s in (0, 1):
        grad_hidden.total(s)
        grad_hidden.far(s, 1)
    for s in (0, 1):
        grad_hidden.direct(s, 1)
    for s in (0, 1):
        projected.joined(s, 0)
    for s in (0, 1):
        grad_hidden.joined(s, 1)
    for s in (0, 1):
        projected.own(s)
    down_rows(6, hid_blocks)
    g_done = grad_hidden.last(gh_ref, lsem.at[4])
    out_rows(0, 2)
    for s in (0, 1):
        projected.total(s)
        projected.far(s, 1)
    for s in (0, 1):
        projected.direct(s, 1)
    for s in (0, 1):
        projected.joined(s, 1)
    out_rows(2, d1 // 256)
    p_done = projected.last(proj_ref, lsem.at[5])
    g_done.wait()
    p_done.wait()
    finish(list(sent))


def keep(*refs):
    loads, stores = [], []
    for source, target, held, pieces in zip(refs[:4], refs[4:8], refs[8:12], (1, 1, 13, 8)):
        count = source.shape[0] // pieces
        for i in range(pieces):
            where, n = pl.ds(i * count, count), len(loads)
            loads.append(pltpu.make_async_copy(source.at[where], held.at[where], refs[12].at[n]))
            stores.append(pltpu.make_async_copy(held.at[where], target.at[where], refs[13].at[n]))
    for load in loads:
        load.start()
    for load, store in zip(loads, stores):
        load.wait()
        store.start()
    for store in stores:
        store.wait()


def local(hidden_act, w_down, w_out, head_grad, token_ratio, pair_slot, segment_id):
    rows, ff = hidden_act.shape
    d1 = w_down.shape[1]
    d2 = w_out.shape[1]
    half1 = d1 // 2
    quarter = 4 * rows

    def reduce_shapes(width):
        half = width // 2
        shapes = [pltpu.VMEM((2, quarter, half), F32)]
        for count in (quarter, rows):
            shapes += [
                pltpu.VMEM((2, 3, count, half), BF),
                pltpu.VMEM((2, count, half), BF),
                pltpu.VMEM((2, 2, count, half), BF),
            ]
        return shapes + [pltpu.VMEM((rows, width), BF)]

    anywhere = pl.BlockSpec(memory_space=pl.ANY)
    copies = 160
    results = pl.pallas_call(
        functools.partial(kernel, rows),
        out_shape=(
            jax.ShapeDtypeStruct((rows, d2), BF),
            jax.ShapeDtypeStruct((rows, ff), BF),
            jax.ShapeDtypeStruct((ff, d1), BF),
            jax.ShapeDtypeStruct((d1, d2), BF),
        ),
        in_specs=[pl.BlockSpec(memory_space=pltpu.VMEM)] * 3 + [anywhere] * 4,
        out_specs=[anywhere] * 4,
        scratch_shapes=[
            pltpu.VMEM((ff, d1), BF),
            pltpu.VMEM((d1, d2), BF),
            pltpu.VMEM((4, 4, rows, ff), BF),
            pltpu.VMEM((4, 4, rows, d2), BF),
            pltpu.VMEM((4, 4, rows, d2), BF),
            pltpu.VMEM((4, 4, 8, 128), F32),
            pltpu.VMEM((2, 4, quarter, 256), F32),
            pltpu.VMEM((2, 4, quarter, 256), F32),
            pltpu.VMEM((2, 4, quarter, 256), F32),
            pltpu.VMEM((2, 4, quarter, 256), BF),
            pltpu.VMEM((2, 3, quarter, 256), BF),
            pltpu.VMEM((2, 4, quarter, half1), BF),
            pltpu.VMEM((2, 4, quarter, half1), BF),
            *reduce_shapes(ff),
            *reduce_shapes(d2),
            pltpu.VMEM((2, 256, d2), BF),
            pltpu.SemaphoreType.DMA((copies,)),
            pltpu.SemaphoreType.DMA((copies,)),
            pltpu.SemaphoreType.DMA((6,)),
            pltpu.SemaphoreType.DMA((2,)),
        ],
        compiler_params=pltpu.CompilerParams(
            collective_id=0, has_side_effects=True, vmem_limit_bytes=62 << 20
        ),
        cost_estimate=pl.CostEstimate(
            flops=6 * 16 * rows * d1 * (ff + d2),
            bytes_accessed=4 * d1 * (ff + d2),
            transcendentals=128,
        ),
    )(
        token_ratio[None], pair_slot[None], segment_id[None], hidden_act, w_down, w_out, head_grad
    )
    return pl.pallas_call(
        keep,
        out_shape=[jax.ShapeDtypeStruct(r.shape, r.dtype) for r in results],
        in_specs=[anywhere] * 4,
        out_specs=[anywhere] * 4,
        scratch_shapes=[pltpu.VMEM(r.shape, r.dtype) for r in results]
        + [pltpu.SemaphoreType.DMA((24,)), pltpu.SemaphoreType.DMA((24,))],
        compiler_params=pltpu.CompilerParams(vmem_limit_bytes=32 << 20),
        cost_estimate=pl.CostEstimate(
            flops=0, bytes_accessed=4 * d1 * (ff + d2), transcendentals=0
        ),
    )(*results)


def solution(mesh):
    placed = (
        P(("ia", "ka"), "ja"),
        P("ja", ("ia", "ka")),
        P(("ia", "ka"), "ja"),
        P(("ia", "ka"), "ja"),
        P(("ia", "ka")),
        P(("ia", "ka")),
        P(("ia", "ka")),
    )
    return jax.shard_map(
        local,
        mesh=mesh,
        in_specs=placed,
        out_specs=(
            P(("ia", "ka"), "ja"),
            P(("ia", "ka"), "ja"),
            P("ja", ("ia", "ka")),
            P(("ia", "ka"), "ja"),
        ),
        check_vma=False,
    )
```

```python
import functools

import jax
import jax.numpy as jnp
from jax import lax
from jax.experimental import pallas as pl
from jax.experimental.pallas import tpu as pltpu
from jax.sharding import PartitionSpec as P

MESH = pl.DeviceIdType.MESH
BF = jnp.bfloat16
F32 = jnp.float32

beta_scale = 0.5


def dot_nt(a, b):
    return lax.dot_general(a, b, (((1,), (1,)), ((), ())), preferred_element_type=F32)


def dot_nn(a, b):
    return lax.dot_general(a, b, (((1,), (0,)), ((), ())), preferred_element_type=F32)


def kernel(
    rows, ratio_ref, slot_ref, segment_ref, hid_ref, wd_ref, wo_ref, hg_ref,
    proj_ref, gh_ref, gd_ref, go_ref,
    wd, wo, hid, hg, cot, tiles,
    sib_out, sib_in, part, xout, xin, gm, dn,
    *bufs,
):
    g_bufs, p_bufs, (stage, ssem, rsem, lsem, osem) = bufs[:8], bufs[8:16], bufs[16:]
    ia, ja, ka = lax.axis_index("ia"), lax.axis_index("ja"), lax.axis_index("ka")
    z, y, x, core = ia * 2 + ka % 2, ka // 2, ja // 2, ja % 2

    def peer(dx=0, dc=0, dy=0, dz=0):
        pz, py, px, pc = (z + dz) % 4, (y + dy) % 4, (x + dx) % 4, (core + dc) % 2
        return (pz // 2, px * 2 + pc, py * 2 + pz % 2)

    count = [0]
    sent = []

    def send(src, dst, **where):
        i = count[0]
        count[0] += 1
        copy = pltpu.make_async_remote_copy(
            src, dst, ssem.at[i], rsem.at[i], device_id=peer(**where), device_id_type=MESH
        )
        copy.start()
        sent.append(copy)
        return copy

    def finish(copies):
        for copy in copies:
            copy.wait_send()
            sent[:] = [other for other in sent if other is not copy]

    def arrive(copies):
        for copy in copies:
            copy.wait_recv()

    near = (2, 1, 3)

    loads = [
        pltpu.make_async_copy(hg_ref, hg.at[0, 0], lsem.at[0]),
        pltpu.make_async_copy(hid_ref, hid.at[0, 0], lsem.at[1]),
        pltpu.make_async_copy(wo_ref, wo, lsem.at[2]),
        pltpu.make_async_copy(wd_ref, wd, lsem.at[3]),
    ]
    for load in loads:
        load.start()

    sign = ((segment_ref[...] & 1) * (1 - 2 * (slot_ref[...] & 1))).astype(F32)
    tiles[0, 0] = jnp.full((8, 128), -1.0, F32)
    tiles[0, 0, 0:1, 0:rows] = sign * ratio_ref[...]
    tiles[0, 0, 1:2, 0:rows] = (slot_ref[...] >> 1).astype(F32)
    tiles[0, 0, 2:3, 0:rows] = sign

    barrier = pltpu.get_barrier_semaphore()
    peers = [dict(dc=1)] + [{a: d} for a in ("dx", "dy", "dz") for d in near]
    for where in peers:
        pl.semaphore_signal(barrier, inc=1, device_id=peer(**where), device_id_type=MESH)
    pl.semaphore_wait(barrier, len(peers))
    for load in loads[:2]:
        load.wait()

    class Gather:
        def __init__(self, full):
            self.full = full
            self.width = full.shape[3] // 2
            self.cut = self.width // 2 // 128 * 128
            self.got = {}

        def columns(self, s, part=None):
            base = s * self.width
            if part is None:
                return pl.ds(base, self.width)
            return pl.ds(base, self.cut) if part == 0 else pl.ds(base + self.cut, self.width - self.cut)

        def slot(self, s, p, q, part=None):
            cols = self.columns(s, part)
            return self.full.at[q, p, :, cols] if s == 0 else self.full.at[p, q, :, cols]

        def along(self, s, second, sign):
            return {("dy", "dz")[(s + second) % 2]: sign}

        def take(self, *key):
            arrive([self.got.pop(key)])

        def start_first(self):
            for sign in (1, -1):
                for s in (0, 1):
                    self.got["p", s, sign] = send(
                        self.slot(s, 0, 0), self.slot(s, -sign % 4, 0), **self.along(s, 0, sign)
                    )

        def across(self, s, p):
            for sign in (1, -1):
                self.got["s", s, p, sign] = send(
                    self.slot(s, p, 0), self.slot(s, p, -sign % 4), **self.along(s, 1, sign)
                )

        def start_second(self):
            for s in (0, 1):
                self.across(s, 0)

        def hand_on(self):
            for sign in (1, -1):
                for s in (0, 1):
                    self.take("p", s, sign)
                    part = 0 if sign == 1 else 1
                    self.got["f", s, sign] = send(
                        self.slot(s, -sign % 4, 0, part), self.slot(s, 2, 0, part), **self.along(s, 0, sign)
                    )
            for sign in (1, -1):
                for s in (0, 1):
                    self.across(s, -sign % 4)

        def far(self):
            for s in (0, 1):
                self.take("f", s, 1)
                self.take("f", s, -1)
                self.across(s, 2)

        def hand_across(self, p):
            for sign in (1, -1):
                for s in (0, 1):
                    self.take("s", s, p, sign)
                    self.take("s", s, p + 1, sign)
                    part = 0 if sign == 1 else 1
                    self.got["g", s, p, sign] = send(
                        self.slot(s, pl.ds(p, 2), -sign % 4, part),
                        self.slot(s, pl.ds(p, 2), 2, part),
                        **self.along(s, 1, sign),
                    )

        def done(self):
            for key in list(self.got):
                self.take(*key)

    grad_rows, hidden_rows = Gather(hg), Gather(hid)
    grad_rows.start_first()
    tile_first = [send(tiles.at[0, 0], tiles.at[0, (4 - d) % 4], dy=d) for d in near]
    grad_rows.start_second()
    hidden_rows.start_first()
    arrive(tile_first)
    tile_second = [send(tiles.at[0], tiles.at[(4 - d) % 4], dz=d) for d in near]
    grad_rows.hand_on()
    grad_rows.far()
    hidden_rows.start_second()
    grad_rows.hand_across(0)
    grad_rows.hand_across(2)

    arrive(tile_second)
    pairs = lax.broadcasted_iota(jnp.int32, (8, 128), 0).astype(F32)

    def add_margin(i, total):
        tile = tiles[i // 4, i % 4]
        return total + jnp.where(tile[1:2] == pairs, tile[0:1], 0.0)

    margin = jnp.sum(
        lax.fori_loop(0, 16, add_margin, jnp.zeros((8, 128), F32)), axis=1, keepdims=True
    )
    weight = -beta_scale * jax.nn.sigmoid(-beta_scale * margin)

    def scale(i, _):
        tile = tiles[i // 4, i % 4]
        line = jnp.sum(jnp.where(tile[1:2] == pairs, weight, 0.0), axis=0, keepdims=True) * tile[2:3]
        coef = jnp.broadcast_to(line, (8, 128)).T[0:rows, 0:1]
        cot[i // 4, i % 4] = (coef * hg[i // 4, i % 4].astype(F32)).astype(BF)
        return 0

    tokens = 16 * rows
    quarter = 4 * rows
    d1 = wd.shape[1]
    half1 = d1 // 2

    class Reduce:
        def __init__(self, term, dest):
            self.term, self.dest = term, dest
            self.swaps, self.moves, self.spread, self.relays = {}, {}, {}, {}

        def fill(self, j, which, ref):
            for n in range(half1 // 256):
                value = self.term(self.base(j), pl.multiple_of(which * half1 + n * 256, 256))
                ref[j, :, :, n * 256:(n + 1) * 256] = value.reshape(4, quarter // 2, 256)

        def base(self, j):
            return 2 * (1 - j)

        def theirs(self, j):
            self.fill(j, 1 - core, sib_out)

        def swap(self, j):
            self.swaps[j] = send(sib_out.at[j], sib_in.at[j], dc=1)

        def mine(self, j):
            self.fill(j, core, part)

        def start(self, j):
            arrive([self.swaps[j]])

            def body(i, _):
                total = part[j, i] + sib_in[j, i]
                part[j, i] = total
                xout[j, i] = total.astype(BF)
                return 0

            lax.fori_loop(0, 4, body, 0)
            self.moves[j] = [send(xout.at[j, (x + d) % 4], xin.at[j, d - 1], dx=d) for d in near]

        def sum(self, j):
            arrive(self.moves[j])
            finish([self.swaps[j]])
            total = part[j, x]
            for d in range(3):
                total = total + xin[j, d].astype(F32)
            self.dest[core, self.base(j) + x // 2, x % 2] = total.astype(BF)
            spot = self.dest.at[core, self.base(j) + x // 2, x % 2]
            self.spread[j] = [send(spot, spot, dx=d) for d in near]

        def relay(self, j):
            arrive(self.spread[j])
            spot = self.dest.at[core, pl.ds(self.base(j), 2)]
            self.relays[j] = send(spot, spot, dc=1)

        def done(self, j):
            arrive([self.relays[j]])
            finish(self.moves[j])

    def back_term(base, start):
        return dot_nt(cot[base:base + 2].reshape(tokens // 2, -1), wo[pl.ds(start, 256), :])

    def down_term(base, start):
        return dot_nn(hid[base:base + 2].reshape(tokens // 2, -1), wd[:, pl.ds(start, 256)])

    sum_back, sum_down = Reduce(back_term, gm), Reduce(down_term, dn)

    grad_rows.done()
    hidden_rows.hand_on()
    lax.fori_loop(0, 16, scale, 0)
    loads[2].wait()
    sum_back.theirs(0)
    sum_back.swap(0)
    hidden_rows.far()
    sum_back.mine(0)
    sum_back.start(0)
    sum_back.theirs(1)
    sum_back.swap(1)
    hidden_rows.hand_across(0)
    sum_back.mine(1)
    sum_back.start(1)
    sum_back.sum(0)
    sum_back.sum(1)
    hidden_rows.hand_across(2)
    sum_back.relay(0)
    loads[3].wait()
    sum_back.done(0)

    def block_rows(full, axis, d, group):
        out = []
        for h in range(2):
            if axis == "z":
                out.append(full[h, d].reshape(quarter, half1))
            else:
                places = range(4) if group is None else range(2 * group, 2 * group + 2)
                first = d % 2 * rows
                out.append(
                    jnp.concatenate([full[h, i, d // 2, first:first + rows] for i in places], axis=0)
                )
        return out

    class Scatter:
        def __init__(self, full, mult, acc, out, relay, inn, out2, relay2, inn2, fin):
            self.full, self.mult, self.acc, self.fin = full, mult, acc, fin
            self.stages = ((out, relay, inn), (out2, relay2, inn2))
            self.width = acc.shape[2]
            cut = self.width // 2 // 128 * 128
            self.parts = (slice(0, cut), slice(cut, self.width))
            self.got = {}

        def axis(self, s, stage):
            return "zy"[(s + stage) % 2]

        def term(self, s, stage, d, part, group=None):
            if stage == 0:
                return self.mult(s, block_rows(self.full, self.axis(s, 0), d, group), part)
            return self.acc[s, d * rows:(d + 1) * rows, part]

        def move(self, key, s, stage, d, part, value, dst, sign, group=None):
            out = self.stages[stage][0]
            cols = pl.ds(part.start, part.stop - part.start)
            count = value.shape[0]
            first = 0 if group is None else group * count
            out[s, d - 1, first:first + count, part] = value.astype(BF)
            lines = pl.ds(first, count)
            copy = send(
                out.at[s, d - 1, lines, cols], dst.at[lines, cols], **{"d" + self.axis(s, stage): sign}
            )
            self.got.setdefault((key, s, stage, sign), []).append(copy)

        def take(self, key, s, stage, sign):
            arrive(self.got.pop((key, s, stage, sign)))

        def far(self, s, stage, group=None):
            relay = self.stages[stage][1]
            for part, sign in zip(self.parts, (1, -1)):
                value = self.term(s, stage, 2, part, group)
                self.move("relay", s, stage, 2, part, value, relay.at[s], sign, group)

        def direct(self, s, stage, signs=(1, -1), group=None):
            inn = self.stages[stage][2]
            for part, sign in zip(self.parts[::-1], (1, -1)):
                if sign in signs:
                    d = sign % 4
                    value = self.term(s, stage, d, part, group)
                    self.move("direct", s, stage, d, part, value, inn.at[s, d // 2], sign, group)

        def joined(self, s, stage):
            relay, inn = self.stages[stage][1:]
            for part, sign in zip(self.parts, (1, -1)):
                d = sign % 4
                value = self.term(s, stage, d, part)
                self.take("relay", s, stage, sign)
                value = value + relay[s, :, part].astype(F32)
                self.move("joined", s, stage, d, part, value, inn.at[s, d // 2], sign)

        def own(self, s):
            for part in self.parts:
                self.acc[s, :, part] = self.term(s, 0, 0, part)

        def total(self, s):
            inn = self.stages[0][2]
            for key in ("direct", "joined"):
                for sign in (1, -1):
                    self.take(key, s, 0, sign)
            self.acc[s] = self.acc[s] + inn[s, 0].astype(F32) + inn[s, 1].astype(F32)

        def last(self, ref, sem):
            inn = self.stages[1][2]
            for s in (0, 1):
                for key in ("direct", "joined"):
                    for sign in (1, -1):
                        self.take(key, s, 1, sign)
                value = self.acc[s, 0:rows] + inn[s, 0].astype(F32) + inn[s, 1].astype(F32)
                self.fin[:, s * self.width:(s + 1) * self.width] = value.astype(BF)
            copy = pltpu.make_async_copy(self.fin, ref, sem)
            copy.start()
            return copy

    ff = wd.shape[0]
    d2 = wo.shape[1]

    def hidden_mult(s, left, part):
        cols = slice(s * (ff // 2) + part.start, s * (ff // 2) + part.stop)
        return dot_nt(left[0], wd[cols, 0:half1]) + dot_nt(left[1], wd[cols, half1:])

    def out_mult(s, left, part):
        cols = slice(s * (d2 // 2) + part.start, s * (d2 // 2) + part.stop)
        return dot_nn(left[0], wo[0:half1, cols]) + dot_nn(left[1], wo[half1:, cols])

    grad_hidden = Scatter(gm, hidden_mult, *g_bufs)
    projected = Scatter(dn, out_mult, *p_bufs)
    hid_blocks = ff // 256

    def weight_rows(left, right, ref, first, last):
        def out_copy(i, slot):
            return pltpu.make_async_copy(
                stage.at[slot, :, 0:ref.shape[1]], ref.at[pl.ds(pl.multiple_of(i * 256, 256), 256)], osem.at[slot]
            )

        def body(i, _):
            slot = i % 2

            @pl.when(i >= first + 2)
            def _():
                out_copy(i - 2, slot).wait()

            value = right(left(i).T)
            stage[slot, :, 0:ref.shape[1]] = value.astype(BF)
            out_copy(i, slot).start()
            return 0

        lax.fori_loop(first, last, body, 0)
        for i in range(max(first, last - 2), last):
            out_copy(i, i % 2).wait()

    def hid_cols(i):
        return hid[:, :, :, pl.ds(pl.multiple_of(i * 256, 256), 256)].reshape(tokens, 256)

    def times_gm(left):
        return jnp.concatenate(
            [dot_nn(left, gm[h].reshape(tokens, half1)) for h in range(2)], axis=1
        )

    per = half1 // 256

    def dn_cols(i):
        return dn[i // per, :, :, :, pl.ds(pl.multiple_of((i % per) * 256, 256), 256)].reshape(tokens, 256)

    def times_cot(left):
        return dot_nn(left, cot[...].reshape(tokens, d2))

    def down_rows(first, last):
        weight_rows(hid_cols, times_gm, gd_ref, first, last)

    def out_rows(first, last):
        weight_rows(dn_cols, times_cot, go_ref, first, last)

    grad_hidden.far(0, 0)
    grad_hidden.far(1, 0, group=1)
    sum_back.relay(1)
    hidden_rows.done()
    sum_down.theirs(0)
    sum_down.swap(0)
    sum_back.done(1)
    sum_down.mine(0)
    sum_down.start(0)
    sum_down.theirs(1)
    sum_down.swap(1)
    sum_down.mine(1)
    sum_down.start(1)
    grad_hidden.far(1, 0, group=0)
    for s in (0, 1):
        grad_hidden.direct(s, 0)
    sum_down.sum(0)
    for s in (0, 1):
        grad_hidden.joined(s, 0)
    sum_down.sum(1)
    for s in (0, 1):
        grad_hidden.own(s)
    sum_down.relay(0)
    down_rows(0, 4)
    sum_down.relay(1)
    sum_down.done(0)
    sum_down.done(1)
    for s in (0, 1):
        projected.far(s, 0)
    for s in (0, 1):
        projected.direct(s, 0)
    for s in (0, 1):
        grad_hidden.total(s)
        grad_hidden.far(s, 1)
    for s in (0, 1):
        grad_hidden.direct(s, 1)
    down_rows(4, 7)
    for s in (0, 1):
        projected.joined(s, 0)
    for s in (0, 1):
        grad_hidden.joined(s, 1)
    for s in (0, 1):
        projected.own(s)
    down_rows(7, hid_blocks)
    g_done = grad_hidden.last(gh_ref, lsem.at[4])
    out_rows(0, 2)
    for s in (0, 1):
        projected.total(s)
        projected.far(s, 1)
    for s in (0, 1):
        projected.direct(s, 1)
    out_rows(2, 3)
    for s in (0, 1):
        projected.joined(s, 1)
    out_rows(3, d1 // 256)
    p_done = projected.last(proj_ref, lsem.at[5])
    g_done.wait()
    p_done.wait()
    finish(list(sent))


def keep(*refs):
    loads, stores = [], []
    for source, target, held, pieces in zip(refs[:4], refs[4:8], refs[8:12], (1, 1, 13, 8)):
        count = source.shape[0] // pieces
        for i in range(pieces):
            where, n = pl.ds(i * count, count), len(loads)
            loads.append(pltpu.make_async_copy(source.at[where], held.at[where], refs[12].at[n]))
            stores.append(pltpu.make_async_copy(held.at[where], target.at[where], refs[13].at[n]))
    for load in loads:
        load.start()
    for load, store in zip(loads, stores):
        load.wait()
        store.start()
    for store in stores:
        store.wait()


def local(hidden_act, w_down, w_out, head_grad, token_ratio, pair_slot, segment_id):
    rows, ff = hidden_act.shape
    d1 = w_down.shape[1]
    d2 = w_out.shape[1]
    half1 = d1 // 2
    quarter = 4 * rows

    def reduce_shapes(width):
        half = width // 2
        shapes = [pltpu.VMEM((2, quarter, half), F32)]
        for count in (quarter, rows):
            shapes += [
                pltpu.VMEM((2, 3, count, half), BF),
                pltpu.VMEM((2, count, half), BF),
                pltpu.VMEM((2, 2, count, half), BF),
            ]
        return shapes + [pltpu.VMEM((rows, width), BF)]

    anywhere = pl.BlockSpec(memory_space=pl.ANY)
    copies = 160
    results = pl.pallas_call(
        functools.partial(kernel, rows),
        out_shape=(
            jax.ShapeDtypeStruct((rows, d2), BF),
            jax.ShapeDtypeStruct((rows, ff), BF),
            jax.ShapeDtypeStruct((ff, d1), BF),
            jax.ShapeDtypeStruct((d1, d2), BF),
        ),
        in_specs=[pl.BlockSpec(memory_space=pltpu.VMEM)] * 3 + [anywhere] * 4,
        out_specs=[anywhere] * 4,
        scratch_shapes=[
            pltpu.VMEM((ff, d1), BF),
            pltpu.VMEM((d1, d2), BF),
            pltpu.VMEM((4, 4, rows, ff), BF),
            pltpu.VMEM((4, 4, rows, d2), BF),
            pltpu.VMEM((4, 4, rows, d2), BF),
            pltpu.VMEM((4, 4, 8, 128), F32),
            pltpu.VMEM((2, 4, quarter // 2, half1), F32),
            pltpu.VMEM((2, 4, quarter // 2, half1), F32),
            pltpu.VMEM((2, 4, quarter // 2, half1), F32),
            pltpu.VMEM((2, 4, quarter // 2, half1), BF),
            pltpu.VMEM((2, 3, quarter // 2, half1), BF),
            pltpu.VMEM((2, 4, 2, quarter // 2, half1), BF),
            pltpu.VMEM((2, 4, 2, quarter // 2, half1), BF),
            *reduce_shapes(ff),
            *reduce_shapes(d2),
            pltpu.VMEM((2, 256, d2), BF),
            pltpu.SemaphoreType.DMA((copies,)),
            pltpu.SemaphoreType.DMA((copies,)),
            pltpu.SemaphoreType.DMA((6,)),
            pltpu.SemaphoreType.DMA((2,)),
        ],
        compiler_params=pltpu.CompilerParams(
            collective_id=0, has_side_effects=True, vmem_limit_bytes=62 << 20
        ),
        cost_estimate=pl.CostEstimate(
            flops=6 * 16 * rows * d1 * (ff + d2),
            bytes_accessed=4 * d1 * (ff + d2),
            transcendentals=128,
        ),
    )(
        token_ratio[None], pair_slot[None], segment_id[None], hidden_act, w_down, w_out, head_grad
    )
    return pl.pallas_call(
        keep,
        out_shape=[jax.ShapeDtypeStruct(r.shape, r.dtype) for r in results],
        in_specs=[anywhere] * 4,
        out_specs=[anywhere] * 4,
        scratch_shapes=[pltpu.VMEM(r.shape, r.dtype) for r in results]
        + [pltpu.SemaphoreType.DMA((24,)), pltpu.SemaphoreType.DMA((24,))],
        compiler_params=pltpu.CompilerParams(vmem_limit_bytes=60 << 20),
        cost_estimate=pl.CostEstimate(
            flops=0, bytes_accessed=4 * d1 * (ff + d2), transcendentals=0
        ),
    )(*results)


def solution(mesh):
    placed = (
        P(("ia", "ka"), "ja"),
        P("ja", ("ia", "ka")),
        P(("ia", "ka"), "ja"),
        P(("ia", "ka"), "ja"),
        P(("ia", "ka")),
        P(("ia", "ka")),
        P(("ia", "ka")),
    )
    return jax.shard_map(
        local,
        mesh=mesh,
        in_specs=placed,
        out_specs=(
            P(("ia", "ka"), "ja"),
            P(("ia", "ka"), "ja"),
            P("ja", ("ia", "ka")),
            P(("ia", "ka"), "ja"),
        ),
        check_vma=False,
    )
```

```python
import functools

import jax
import jax.numpy as jnp
from jax import lax
from jax.experimental import pallas as pl
from jax.experimental.pallas import tpu as pltpu
from jax.sharding import PartitionSpec as P

MESH = pl.DeviceIdType.MESH
BF = jnp.bfloat16
F32 = jnp.float32

beta_scale = 0.5


def dot_nt(a, b):
    return lax.dot_general(a, b, (((1,), (1,)), ((), ())), preferred_element_type=F32)


def dot_nn(a, b):
    return lax.dot_general(a, b, (((1,), (0,)), ((), ())), preferred_element_type=F32)


def kernel(
    rows, ratio_ref, slot_ref, segment_ref, hid_ref, wd_ref, wo_ref, hg_ref,
    proj_ref, gh_ref, gd_ref, go_ref,
    wd, wo, hid, hg, cot, tiles,
    sib_out, sib_in, part, xout, xin, gm, dn,
    *bufs,
):
    g_bufs, p_bufs, (stage, ssem, rsem, lsem, osem) = bufs[:8], bufs[8:16], bufs[16:]
    ia, ja, ka = lax.axis_index("ia"), lax.axis_index("ja"), lax.axis_index("ka")
    z, y, x, core = ia * 2 + ka % 2, ka // 2, ja // 2, ja % 2

    def peer(dx=0, dc=0, dy=0, dz=0):
        pz, py, px, pc = (z + dz) % 4, (y + dy) % 4, (x + dx) % 4, (core + dc) % 2
        return (pz // 2, px * 2 + pc, py * 2 + pz % 2)

    count = [0]
    sent = []

    def send(src, dst, **where):
        i = count[0]
        count[0] += 1
        copy = pltpu.make_async_remote_copy(
            src, dst, ssem.at[i], rsem.at[i], device_id=peer(**where), device_id_type=MESH
        )
        copy.start()
        sent.append(copy)
        return copy

    def finish(copies):
        for copy in copies:
            copy.wait_send()
            sent[:] = [other for other in sent if other is not copy]

    def arrive(copies):
        for copy in copies:
            copy.wait_recv()

    near = (2, 1, 3)

    loads = [
        pltpu.make_async_copy(hg_ref, hg.at[0, 0], lsem.at[0]),
        pltpu.make_async_copy(hid_ref, hid.at[0, 0], lsem.at[1]),
        pltpu.make_async_copy(wo_ref, wo, lsem.at[2]),
        pltpu.make_async_copy(wd_ref, wd, lsem.at[3]),
    ]
    for load in loads[:2]:
        load.start()

    sign = ((segment_ref[...] & 1) * (1 - 2 * (slot_ref[...] & 1))).astype(F32)
    tiles[0, 0] = jnp.full((8, 128), -1.0, F32)
    tiles[0, 0, 0:1, 0:rows] = sign * ratio_ref[...]
    tiles[0, 0, 1:2, 0:rows] = (slot_ref[...] >> 1).astype(F32)
    tiles[0, 0, 2:3, 0:rows] = sign

    barrier = pltpu.get_barrier_semaphore()
    peers = [dict(dc=1)] + [{a: d} for a in ("dx", "dy", "dz") for d in near]
    for where in peers:
        pl.semaphore_signal(barrier, inc=1, device_id=peer(**where), device_id_type=MESH)
    pl.semaphore_wait(barrier, len(peers))
    for load in loads[:2]:
        load.wait()
    for load in loads[2:]:
        load.start()

    class Gather:
        def __init__(self, full):
            self.full = full
            self.width = full.shape[3] // 2
            self.cut = self.width // 2 // 128 * 128
            self.got = {}

        def columns(self, s, part=None):
            base = s * self.width
            if part is None:
                return pl.ds(base, self.width)
            return pl.ds(base, self.cut) if part == 0 else pl.ds(base + self.cut, self.width - self.cut)

        def slot(self, s, p, q, part=None):
            cols = self.columns(s, part)
            return self.full.at[q, p, :, cols] if s == 0 else self.full.at[p, q, :, cols]

        def along(self, s, second, sign):
            return {("dy", "dz")[(s + second) % 2]: sign}

        def take(self, *key):
            arrive([self.got.pop(key)])

        def start_first(self):
            for sign in (1, -1):
                for s in (0, 1):
                    self.got["p", s, sign] = send(
                        self.slot(s, 0, 0), self.slot(s, -sign % 4, 0), **self.along(s, 0, sign)
                    )

        def across(self, s, p):
            for sign in (1, -1):
                self.got["s", s, p, sign] = send(
                    self.slot(s, p, 0), self.slot(s, p, -sign % 4), **self.along(s, 1, sign)
                )

        def start_second(self):
            for s in (0, 1):
                self.across(s, 0)

        def hand_on(self):
            for sign in (1, -1):
                for s in (0, 1):
                    self.take("p", s, sign)
                    part = 0 if sign == 1 else 1
                    self.got["f", s, sign] = send(
                        self.slot(s, -sign % 4, 0, part), self.slot(s, 2, 0, part), **self.along(s, 0, sign)
                    )
            for sign in (1, -1):
                for s in (0, 1):
                    self.across(s, -sign % 4)

        def far(self):
            for s in (0, 1):
                self.take("f", s, 1)
                self.take("f", s, -1)
                self.across(s, 2)

        def hand_across(self, p):
            for sign in (1, -1):
                for s in (0, 1):
                    self.take("s", s, p, sign)
                    self.take("s", s, p + 1, sign)
                    part = 0 if sign == 1 else 1
                    self.got["g", s, p, sign] = send(
                        self.slot(s, pl.ds(p, 2), -sign % 4, part),
                        self.slot(s, pl.ds(p, 2), 2, part),
                        **self.along(s, 1, sign),
                    )

        def done(self):
            for key in list(self.got):
                self.take(*key)

    grad_rows, hidden_rows = Gather(hg), Gather(hid)
    grad_rows.start_first()
    tile_first = [send(tiles.at[0, 0], tiles.at[0, (4 - d) % 4], dy=d) for d in near]
    grad_rows.start_second()
    hidden_rows.start_first()
    arrive(tile_first)
    tile_second = [send(tiles.at[0], tiles.at[(4 - d) % 4], dz=d) for d in near]
    grad_rows.hand_on()
    grad_rows.far()
    hidden_rows.start_second()
    grad_rows.hand_across(0)
    grad_rows.hand_across(2)

    arrive(tile_second)
    pairs = lax.broadcasted_iota(jnp.int32, (8, 128), 0).astype(F32)

    def add_margin(i, total):
        tile = tiles[i // 4, i % 4]
        return total + jnp.where(tile[1:2] == pairs, tile[0:1], 0.0)

    margin = jnp.sum(
        lax.fori_loop(0, 16, add_margin, jnp.zeros((8, 128), F32)), axis=1, keepdims=True
    )
    weight = -beta_scale * jax.nn.sigmoid(-beta_scale * margin)

    def scale(q, p):
        tile = tiles[q, p]
        line = jnp.sum(jnp.where(tile[1:2] == pairs, weight, 0.0), axis=0, keepdims=True) * tile[2:3]
        coef = jnp.broadcast_to(line, (8, 128)).T[0:rows, 0:1]
        cot[q, p] = (coef * hg[q, p].astype(F32)).astype(BF)

    def scale_near(i, _):
        q, p = i // 3, i % 3
        scale(q + q // 2, p + p // 2)
        return 0

    def scale_far(i, _):
        other = lax.max(i - 4, 0)
        across = lax.min(i // 4, 1)
        scale(2 + across * (other + other // 2 - 2), i + across * (2 - i))
        return 0

    tokens = 16 * rows
    quarter = 4 * rows
    d1 = wd.shape[1]
    half1 = d1 // 2

    class Reduce:
        def __init__(self, term, dest):
            self.term, self.dest = term, dest
            self.swaps, self.moves, self.spread, self.relays = {}, {}, {}, {}

        def fill(self, j, which, ref):
            for n in range(half1 // 256):
                value = self.term(self.base(j), pl.multiple_of(which * half1 + n * 256, 256))
                ref[j, :, :, n * 256:(n + 1) * 256] = value.reshape(4, quarter // 2, 256)

        def base(self, j):
            return 2 * (1 - j)

        def theirs(self, j):
            self.fill(j, 1 - core, sib_out)

        def swap(self, j):
            self.swaps[j] = send(sib_out.at[j], sib_in.at[j], dc=1)

        def mine(self, j):
            self.fill(j, core, part)

        def start(self, j):
            arrive([self.swaps[j]])

            def body(i, _):
                total = part[j, i] + sib_in[j, i]
                part[j, i] = total
                xout[j, i] = total.astype(BF)
                return 0

            lax.fori_loop(0, 4, body, 0)
            self.moves[j] = [send(xout.at[j, (x + d) % 4], xin.at[j, d - 1], dx=d) for d in near]

        def sum(self, j):
            arrive(self.moves[j])
            finish([self.swaps[j]])
            total = part[j, x]
            for d in range(3):
                total = total + xin[j, d].astype(F32)
            self.dest[core, self.base(j) + x // 2, x % 2] = total.astype(BF)
            spot = self.dest.at[core, self.base(j) + x // 2, x % 2]
            self.spread[j] = [send(spot, spot, dx=d) for d in near]

        def relay(self, j):
            arrive(self.spread[j])
            spot = self.dest.at[core, pl.ds(self.base(j), 2)]
            self.relays[j] = send(spot, spot, dc=1)

        def done(self, j):
            arrive([self.relays[j]])
            finish(self.moves[j])

    def back_term(base, start):
        return dot_nt(cot[base:base + 2].reshape(tokens // 2, -1), wo[pl.ds(start, 256), :])

    def down_term(base, start):
        return dot_nn(hid[base:base + 2].reshape(tokens // 2, -1), wd[:, pl.ds(start, 256)])

    sum_back, sum_down = Reduce(back_term, gm), Reduce(down_term, dn)

    lax.fori_loop(0, 9, scale_near, 0)
    grad_rows.done()
    hidden_rows.hand_on()
    lax.fori_loop(0, 7, scale_far, 0)
    loads[2].wait()
    sum_back.theirs(0)
    sum_back.swap(0)
    hidden_rows.far()
    sum_back.mine(0)
    sum_back.start(0)
    sum_back.theirs(1)
    sum_back.swap(1)
    hidden_rows.hand_across(0)
    sum_back.mine(1)
    sum_back.start(1)
    sum_back.sum(0)
    sum_back.sum(1)
    hidden_rows.hand_across(2)
    sum_back.relay(0)
    loads[3].wait()
    sum_back.done(0)

    def block_rows(full, axis, d, group):
        out = []
        for h in range(2):
            if axis == "z":
                out.append(full[h, d].reshape(quarter, half1))
            else:
                places = range(4) if group is None else range(2 * group, 2 * group + 2)
                first = d % 2 * rows
                out.append(
                    jnp.concatenate([full[h, i, d // 2, first:first + rows] for i in places], axis=0)
                )
        return out

    class Scatter:
        def __init__(self, full, mult, acc, out, relay, inn, out2, relay2, inn2, fin):
            self.full, self.mult, self.acc, self.fin = full, mult, acc, fin
            self.stages = ((out, relay, inn), (out2, relay2, inn2))
            self.width = acc.shape[2]
            cut = self.width // 2 // 128 * 128
            self.parts = (slice(0, cut), slice(cut, self.width))
            self.got = {}

        def axis(self, s, stage):
            return "zy"[(s + stage) % 2]

        def term(self, s, stage, d, part, group=None):
            if stage == 0:
                return self.mult(s, block_rows(self.full, self.axis(s, 0), d, group), part)
            return self.acc[s, d * rows:(d + 1) * rows, part]

        def move(self, key, s, stage, d, part, value, dst, sign, group=None):
            out = self.stages[stage][0]
            cols = pl.ds(part.start, part.stop - part.start)
            count = value.shape[0]
            first = 0 if group is None else group * count
            out[s, d - 1, first:first + count, part] = value.astype(BF)
            lines = pl.ds(first, count)
            copy = send(
                out.at[s, d - 1, lines, cols], dst.at[lines, cols], **{"d" + self.axis(s, stage): sign}
            )
            self.got.setdefault((key, s, stage, sign), []).append(copy)

        def take(self, key, s, stage, sign):
            arrive(self.got.pop((key, s, stage, sign)))

        def far(self, s, stage, group=None):
            relay = self.stages[stage][1]
            for part, sign in zip(self.parts, (1, -1)):
                value = self.term(s, stage, 2, part, group)
                self.move("relay", s, stage, 2, part, value, relay.at[s], sign, group)

        def direct(self, s, stage, signs=(1, -1), group=None):
            inn = self.stages[stage][2]
            for part, sign in zip(self.parts[::-1], (1, -1)):
                if sign in signs:
                    d = sign % 4
                    value = self.term(s, stage, d, part, group)
                    self.move("direct", s, stage, d, part, value, inn.at[s, d // 2], sign, group)

        def joined(self, s, stage):
            relay, inn = self.stages[stage][1:]
            for part, sign in zip(self.parts, (1, -1)):
                d = sign % 4
                value = self.term(s, stage, d, part)
                self.take("relay", s, stage, sign)
                value = value + relay[s, :, part].astype(F32)
                self.move("joined", s, stage, d, part, value, inn.at[s, d // 2], sign)

        def straight(self, s):
            out, relay, inn = self.stages[1]
            for d, dst in ((2, relay.at[s]), (1, inn.at[s, 0]), (3, inn.at[s, 1])):
                out[s, d - 1] = self.acc[s, d * rows:(d + 1) * rows].astype(BF)
                copy = send(out.at[s, d - 1], dst, **{"d" + self.axis(s, 1): d})
                self.got.setdefault(("straight", s), []).append(copy)

        def own(self, s):
            for part in self.parts:
                self.acc[s, :, part] = self.term(s, 0, 0, part)

        def total(self, s):
            inn = self.stages[0][2]
            for key in ("direct", "joined"):
                for sign in (1, -1):
                    self.take(key, s, 0, sign)
            self.acc[s] = self.acc[s] + inn[s, 0].astype(F32) + inn[s, 1].astype(F32)

        def last(self, ref, sem):
            inn = self.stages[1][2]
            for s in (0, 1):
                value = self.acc[s, 0:rows]
                if ("straight", s) in self.got:
                    arrive(self.got.pop(("straight", s)))
                    value = value + self.stages[1][1][s].astype(F32)
                else:
                    for key in ("direct", "joined"):
                        for sign in (1, -1):
                            self.take(key, s, 1, sign)
                value = value + inn[s, 0].astype(F32) + inn[s, 1].astype(F32)
                self.fin[:, s * self.width:(s + 1) * self.width] = value.astype(BF)
            copy = pltpu.make_async_copy(self.fin, ref, sem)
            copy.start()
            return copy

    ff = wd.shape[0]
    d2 = wo.shape[1]

    def hidden_mult(s, left, part):
        cols = slice(s * (ff // 2) + part.start, s * (ff // 2) + part.stop)
        return dot_nt(left[0], wd[cols, 0:half1]) + dot_nt(left[1], wd[cols, half1:])

    def out_mult(s, left, part):
        cols = slice(s * (d2 // 2) + part.start, s * (d2 // 2) + part.stop)
        return dot_nn(left[0], wo[0:half1, cols]) + dot_nn(left[1], wo[half1:, cols])

    grad_hidden = Scatter(gm, hidden_mult, *g_bufs)
    projected = Scatter(dn, out_mult, *p_bufs)
    hid_blocks = ff // 256

    def weight_rows(left, right, ref, first, last):
        def out_copy(i, slot):
            return pltpu.make_async_copy(
                stage.at[slot, :, 0:ref.shape[1]], ref.at[pl.ds(pl.multiple_of(i * 256, 256), 256)], osem.at[slot]
            )

        def body(i, _):
            slot = i % 2

            @pl.when(i >= first + 2)
            def _():
                out_copy(i - 2, slot).wait()

            value = right(left(i).T)
            stage[slot, :, 0:ref.shape[1]] = value.astype(BF)
            out_copy(i, slot).start()
            return 0

        lax.fori_loop(first, last, body, 0)
        for i in range(max(first, last - 2), last):
            out_copy(i, i % 2).wait()

    def hid_cols(i):
        return hid[:, :, :, pl.ds(pl.multiple_of(i * 256, 256), 256)].reshape(tokens, 256)

    def times_gm(left):
        return jnp.concatenate(
            [dot_nn(left, gm[h].reshape(tokens, half1)) for h in range(2)], axis=1
        )

    per = half1 // 256

    def dn_cols(i):
        return dn[i // per, :, :, :, pl.ds(pl.multiple_of((i % per) * 256, 256), 256)].reshape(tokens, 256)

    def times_cot(left):
        return dot_nn(left, cot[...].reshape(tokens, d2))

    def down_rows(first, last):
        weight_rows(hid_cols, times_gm, gd_ref, first, last)

    def out_rows(first, last):
        weight_rows(dn_cols, times_cot, go_ref, first, last)

    grad_hidden.far(0, 0)
    grad_hidden.far(1, 0, group=1)
    sum_back.relay(1)
    hidden_rows.done()
    sum_down.theirs(0)
    sum_down.swap(0)
    sum_back.done(1)
    sum_down.mine(0)
    sum_down.start(0)
    sum_down.theirs(1)
    sum_down.swap(1)
    sum_down.mine(1)
    sum_down.start(1)
    grad_hidden.far(1, 0, group=0)
    for s in (0, 1):
        grad_hidden.direct(s, 0)
    sum_down.sum(0)
    for s in (0, 1):
        grad_hidden.joined(s, 0)
    sum_down.sum(1)
    for s in (0, 1):
        grad_hidden.own(s)
    sum_down.relay(0)
    down_rows(0, 4)
    sum_down.relay(1)
    sum_down.done(0)
    sum_down.done(1)
    for s in (0, 1):
        projected.far(s, 0)
    for s in (0, 1):
        projected.direct(s, 0)
    for s in (0, 1):
        grad_hidden.total(s)
        grad_hidden.far(s, 1)
    for s in (0, 1):
        grad_hidden.direct(s, 1)
    down_rows(4, 7)
    for s in (0, 1):
        projected.joined(s, 0)
    for s in (0, 1):
        grad_hidden.joined(s, 1)
    for s in (0, 1):
        projected.own(s)
    down_rows(7, hid_blocks)
    g_done = grad_hidden.last(gh_ref, lsem.at[4])
    for s in (0, 1):
        projected.total(s)
        projected.straight(s)
    out_rows(0, d1 // 256)
    p_done = projected.last(proj_ref, lsem.at[5])
    g_done.wait()
    p_done.wait()
    finish(list(sent))


def keep(*refs):
    loads, stores = [], []
    for source, target, held, pieces in zip(refs[:4], refs[4:8], refs[8:12], (1, 1, 13, 8)):
        count = source.shape[0] // pieces
        for i in range(pieces):
            where, n = pl.ds(i * count, count), len(loads)
            loads.append(pltpu.make_async_copy(source.at[where], held.at[where], refs[12].at[n]))
            stores.append(pltpu.make_async_copy(held.at[where], target.at[where], refs[13].at[n]))
    for load in loads:
        load.start()
    for load, store in zip(loads, stores):
        load.wait()
        store.start()
    for store in stores:
        store.wait()


def local(hidden_act, w_down, w_out, head_grad, token_ratio, pair_slot, segment_id):
    rows, ff = hidden_act.shape
    d1 = w_down.shape[1]
    d2 = w_out.shape[1]
    half1 = d1 // 2
    quarter = 4 * rows

    def reduce_shapes(width):
        half = width // 2
        shapes = [pltpu.VMEM((2, quarter, half), F32)]
        for count in (quarter, rows):
            shapes += [
                pltpu.VMEM((2, 3, count, half), BF),
                pltpu.VMEM((2, count, half), BF),
                pltpu.VMEM((2, 2, count, half), BF),
            ]
        return shapes + [pltpu.VMEM((rows, width), BF)]

    anywhere = pl.BlockSpec(memory_space=pl.ANY)
    copies = 160
    results = pl.pallas_call(
        functools.partial(kernel, rows),
        out_shape=(
            jax.ShapeDtypeStruct((rows, d2), BF),
            jax.ShapeDtypeStruct((rows, ff), BF),
            jax.ShapeDtypeStruct((ff, d1), BF),
            jax.ShapeDtypeStruct((d1, d2), BF),
        ),
        in_specs=[pl.BlockSpec(memory_space=pltpu.VMEM)] * 3 + [anywhere] * 4,
        out_specs=[anywhere] * 4,
        scratch_shapes=[
            pltpu.VMEM((ff, d1), BF),
            pltpu.VMEM((d1, d2), BF),
            pltpu.VMEM((4, 4, rows, ff), BF),
            pltpu.VMEM((4, 4, rows, d2), BF),
            pltpu.VMEM((4, 4, rows, d2), BF),
            pltpu.VMEM((4, 4, 8, 128), F32),
            pltpu.VMEM((2, 4, quarter // 2, half1), F32),
            pltpu.VMEM((2, 4, quarter // 2, half1), F32),
            pltpu.VMEM((2, 4, quarter // 2, half1), F32),
            pltpu.VMEM((2, 4, quarter // 2, half1), BF),
            pltpu.VMEM((2, 3, quarter // 2, half1), BF),
            pltpu.VMEM((2, 4, 2, quarter // 2, half1), BF),
            pltpu.VMEM((2, 4, 2, quarter // 2, half1), BF),
            *reduce_shapes(ff),
            *reduce_shapes(d2),
            pltpu.VMEM((2, 256, d2), BF),
            pltpu.SemaphoreType.DMA((copies,)),
            pltpu.SemaphoreType.DMA((copies,)),
            pltpu.SemaphoreType.DMA((6,)),
            pltpu.SemaphoreType.DMA((2,)),
        ],
        compiler_params=pltpu.CompilerParams(
            collective_id=0, has_side_effects=True, vmem_limit_bytes=62 << 20
        ),
        cost_estimate=pl.CostEstimate(
            flops=6 * 16 * rows * d1 * (ff + d2),
            bytes_accessed=4 * d1 * (ff + d2),
            transcendentals=128,
        ),
    )(
        token_ratio[None], pair_slot[None], segment_id[None], hidden_act, w_down, w_out, head_grad
    )
    return pl.pallas_call(
        keep,
        out_shape=[jax.ShapeDtypeStruct(r.shape, r.dtype) for r in results],
        in_specs=[anywhere] * 4,
        out_specs=[anywhere] * 4,
        scratch_shapes=[pltpu.VMEM(r.shape, r.dtype) for r in results]
        + [pltpu.SemaphoreType.DMA((24,)), pltpu.SemaphoreType.DMA((24,))],
        compiler_params=pltpu.CompilerParams(vmem_limit_bytes=60 << 20),
        cost_estimate=pl.CostEstimate(
            flops=0, bytes_accessed=4 * d1 * (ff + d2), transcendentals=0
        ),
    )(*results)


def solution(mesh):
    placed = (
        P(("ia", "ka"), "ja"),
        P("ja", ("ia", "ka")),
        P(("ia", "ka"), "ja"),
        P(("ia", "ka"), "ja"),
        P(("ia", "ka")),
        P(("ia", "ka")),
        P(("ia", "ka")),
    )
    return jax.shard_map(
        local,
        mesh=mesh,
        in_specs=placed,
        out_specs=(
            P(("ia", "ka"), "ja"),
            P(("ia", "ka"), "ja"),
            P("ja", ("ia", "ka")),
            P(("ia", "ka"), "ja"),
        ),
        check_vma=False,
    )
```
